1024 devices in a mesh: surf: 128 (over y, x, z_lo), depth: 8 (over z_hi, core).
Axes of the slice: x: 4, y: 8, z: 16 (z_hi: 4, z_lo: 4; z = z_hi * 4 + z_lo), core: 2. Of those that a mesh axis runs over, the one named last changes fastest.
Arguments:
- temp_old: float32 [64, 2048, 128], P('depth', 'surf'), may hold values from 0.5 to 2
- virgin: float32 [64, 2048, 128], P('depth', 'surf'), may hold values from 0.2 to 1
- zone: int32 [64, 2048, 128], P('depth', 'surf'), may hold values from 0 to 7, as said below
- zone_props: float32 [4, 8], replicated, as said below
- gas_flux: bfloat16 [16384, 128], P('surf'), may hold values from -6 to 6
- gas_owner: int32 [16384, 1], P('surf'), may hold values from 0 to 127; in each aligned block of 128 rows (0 to 127, 128 to 255, ...) at most 2 rows name the same one
- gas_cell: int32 [16384], P('surf'), may hold values from 0 to 15
Outputs:
- increment: float32 [64, 2048, 128], P('depth', 'surf')
The draws below stay inside these ranges and needn't reach their ends.
Inputs may be any that keep to these rules, and one draw needn't show every extreme that they name: `gas_owner`: in the rows of one device at most 2 name the same owner. The zone is the same over aligned blocks of 8 cells through the thickness by 8 cells along the first surface dimension. `zone_props`: all entries positive.
All inputs are finite; a program needn't handle non-finite values.
Results may differ from the reference program's by a relative error of at most 0.0003.
Values may be sent and summed in bfloat16 or wider, within the bound.
A program may use at most 32 MiB of HBM per device.

```python
import math
import jax
import jax.numpy as jnp
import numpy as np
from jax import lax

CX = 16
NY = 128
ZONES = 8
CAP = 2
LEVELS = 4
CYCLES = 2
GAS_DEV = 128
NZ = 64
NX = 2048
GAS_ROWS = 16384
N_SURF = 128


def draw_zone(key, part):
    key = jax.random.fold_in(key, 5)
    block_len = 8
    coarse = jax.random.randint(key, (NZ // block_len, NX // block_len, NY), 0, ZONES)
    return jnp.repeat(jnp.repeat(coarse, block_len, axis=0), block_len, axis=1).astype(jnp.int32)


def draw_zone_props(key, part):
    key = jax.random.fold_in(key, 7)
    unit = jax.random.uniform(key, (4, ZONES), jnp.float32)
    low_end = jnp.array([300.0, 0.3, 0.3, 0.3], jnp.float32)[:, None]
    high_end = jnp.array([3000.0, 3.0, 3.0, 3.0], jnp.float32)[:, None]
    logged = jnp.log(low_end) + unit * (jnp.log(high_end) - jnp.log(low_end))
    return jnp.exp(logged).astype(jnp.float32)


def set_ends(values, key, low, largest):
    longest = values.shape.index(max(values.shape))
    spots = []
    for shift in (0, 1):
        where = [jax.random.randint(jax.random.fold_in(key, axis), (), 0, length) for axis, length in enumerate(values.shape)]
        where[longest] = (where[longest] + shift) % values.shape[longest]
        spots.append(tuple(where))
    return values.at[spots[0]].set(low).at[spots[1]].set(largest)


def steps_of(stream_key, dims, shards, low, top_value):
    factor_of, own = 1.0, jax.random.fold_in(stream_key, 6)
    for position, parts in shards:
        draws = jnp.exp(jax.random.uniform(jax.random.fold_in(own, position), (parts,), jnp.float32, low / len(shards), top_value / len(shards)))
        factor_of = factor_of * jnp.repeat(draws, dims[position] // parts).reshape([-1 if axis == position else 1 for axis in range(len(dims))])
    return factor_of


def assign_block(key, own, number, rows, number_of, top, reach, skew):
    sequence = jax.random.permutation(key, number_of)
    packed, common = portions_of(number_of, rows * top, reach, skew, True), portions_of(number_of, rows * top, reach, skew, False)
    places = jnp.arange(number_of)

    def named(lengths, offset_by):
        used = int((lengths > 0).sum())
        fixed = max(1, used // 4)
        shifted = fixed + (places - fixed + offset_by * (used - fixed)) % max(1, number_of - fixed)
        return jnp.zeros((number_of,), jnp.int32).at[sequence[jnp.where(places < fixed, places, shifted)]].set(jnp.asarray(lengths, jnp.int32))

    lengths = jnp.where(number % 4 == 0, named(packed, number // 4), named(common, number - number // 4 - 1))
    mixed = jax.random.permutation(jax.random.fold_in(own, 3), number_of)
    giver, sink = mixed[0:number_of // 2 * 2:2], mixed[1:number_of // 2 * 2:2]
    room = jnp.minimum(lengths[giver] - 1, reach - lengths[sink]) // 2
    room = jnp.where((giver == sequence[0]) | (sink == sequence[0]) | (lengths[sink] == 0), 0, jnp.maximum(room, 0))
    shifted = jax.random.randint(jax.random.fold_in(own, 4), (number_of // 2,), 0, 1 << 20) % (room + 1)
    lengths = lengths.at[giver].add(-shifted).at[sink].add(shifted)
    labels = jnp.searchsorted(jnp.cumsum(lengths), jnp.arange(rows * top), side="right").astype(jnp.int32)
    grid = labels.reshape(top, rows).T
    grid = grid[jax.random.permutation(jax.random.fold_in(own, 1), rows)]
    offset_by = jax.random.randint(jax.random.fold_in(own, 2), (rows, 1), 0, top)
    return jnp.take_along_axis(grid, (jnp.arange(top)[None, :] + offset_by) % top, axis=1)


def portions_of(amount, total, limit, slope, full):
    weights = [(1 << 20) // math.isqrt(rank ** slope) + 1 for rank in range(1, amount + 1)]
    largest = limit if full else min(limit, max(-(-total // amount), total * weights[0] // sum(weights)))
    least = 1 if total - largest >= amount - 1 else 0
    counts, rest = [largest] + [least] * (amount - 1), total - largest - least * (amount - 1)
    while rest > 0:
        movable = [i for i in range(1, amount) if counts[i] < largest] or [i for i in range(1, amount) if counts[i] < limit]
        pool, left = sum([weights[i] for i in movable]), rest
        for i in movable:
            extra = min(limit - counts[i], max(1, left * weights[i] // pool), rest)
            counts[i] = counts[i] + extra
            rest = rest - extra
    return np.array(counts)


def centred(key, extent, deviation, most, shards=(), dtype=jnp.bfloat16):
    result = deviation * jax.random.normal(key, extent, jnp.float32)
    if shards:
        result = result * steps_of(key, extent, shards, -0.22, 0.18)
    return jnp.clip(result, -most, most).astype(dtype)


def setup_inputs(seed: int = 0) -> dict:
    key_of = jax.random.split(jax.random.key(seed), 8)
    temp_old = jnp.clip(0.5 + 1.5 * jax.random.uniform(key_of[0], (NZ, NX, NY), jnp.float32) ** steps_of(key_of[0], (NZ, NX, NY), ((0, 8), (1, 128)), -0.2, 0.2), 0.5, 2.0)
    virgin = jnp.clip(0.2 + 0.8 * jax.random.uniform(key_of[1], (NZ, NX, NY), jnp.float32) ** steps_of(key_of[1], (NZ, NX, NY), ((0, 8), (1, 128)), -0.2, 0.2), 0.2, 1.0)
    zone = draw_zone(jax.random.fold_in(key_of[7], 71), 0)
    zone_props = draw_zone_props(jax.random.fold_in(key_of[7], 71), 0)
    gas_flux = centred(key_of[4], (GAS_ROWS, NY), 1.0, 6.0, ((0, 128),))
    gas_owner_keys = jax.random.split(jax.random.fold_in(key_of[5], 1), GAS_ROWS // GAS_DEV)
    gas_owner_turns = jax.random.permutation(jax.random.fold_in(key_of[5], 3), GAS_ROWS // GAS_DEV)
    gas_owner = jax.vmap(lambda own, number: assign_block(jax.random.fold_in(key_of[5], 2), own, number, GAS_DEV, N_SURF, 1, CAP, 2))(gas_owner_keys, gas_owner_turns).reshape((GAS_ROWS, 1))
    gas_cell = set_ends(jax.random.randint(key_of[6], (GAS_ROWS,), 0, CX), jax.random.fold_in(key_of[6], 1), 0, CX - 1).astype(jnp.int32)
    return {"temp_old": temp_old, "virgin": virgin, "zone": zone, "zone_props": zone_props, "gas_flux": gas_flux, "gas_owner": gas_owner, "gas_cell": gas_cell}


omega_weight = 0.8


def weights_from_padded(padded_z, padded_x, cond_y, factor):
    faces_z = 0.5 * (padded_z[:-1] + padded_z[1:]) * factor
    faces_x = 0.5 * (padded_x[:, :-1] + padded_x[:, 1:]) * factor
    padded_y = jnp.pad(cond_y, ((0, 0), (0, 0), (1, 1)))
    faces_y = 0.5 * (padded_y[:, :, :-1] + padded_y[:, :, 1:])
    return faces_z[:-1], faces_z[1:], faces_x[:, :-1], faces_x[:, 1:], faces_y[:, :, :-1], faces_y[:, :, 1:]


def build_operator(diagonal, weights):
    lower_face, upper_face, west_face, east_face, south_face, north_face = weights
    centre = diagonal + lower_face + upper_face + west_face + east_face + south_face + north_face
    return (centre, lower_face, upper_face, west_face, east_face, south_face, north_face)


def operate(padded, operator):
    centre, lower_face, upper_face, west_face, east_face, south_face, north_face = operator
    middle = padded[1:-1, 1:-1]
    along_y = jnp.pad(middle, ((0, 0), (0, 0), (1, 1)))
    return (centre * middle - lower_face * padded[:-2, 1:-1] - upper_face * padded[2:, 1:-1]
            - west_face * padded[1:-1, :-2] - east_face * padded[1:-1, 2:]
            - south_face * along_y[:, :, :-2] - north_face * along_y[:, :, 2:])


def restrict(field):
    depth_len, width_len, cross_len = field.shape
    return field.reshape(depth_len // 2, 2, width_len // 2, 2, cross_len).mean(axis=(1, 3))


def prolong(field):
    return jnp.repeat(jnp.repeat(field, 2, axis=0), 2, axis=1)


def line_solve(centre, lower_face, upper_face, rhs):
    zeros = jnp.zeros(rhs.shape[1:], jnp.float32)

    def forward(carry, rows):
        ratio_prev, value_prev = carry
        centre_row, lower_row, upper_row, rhs_row = rows
        denom = centre_row - lower_row * ratio_prev
        ratio = upper_row / denom
        value = (rhs_row + lower_row * value_prev) / denom
        return (ratio, value), (ratio, value)

    unused, (ratios, values) = lax.scan(forward, (zeros, zeros), (centre, lower_face, upper_face, rhs))

    def backward(later, rows):
        ratio, value = rows
        current = value + ratio * later
        return current, current

    unused_two, solved = lax.scan(backward, zeros, (ratios, values), reverse=True)
    return solved


def pad_sides(field):
    return jnp.pad(field, ((1, 1), (1, 1), (0, 0)))


def vcycle(operators, level, guess, rhs):
    operator = operators[level]
    if level == len(operators) - 1:
        return line_solve(operator[0], operator[1], operator[2], rhs)
    if guess is None:
        field = omega_weight * rhs / operator[0]
    else:
        field = guess + omega_weight * (rhs - operate(pad_sides(guess), operator)) / operator[0]
    residual = rhs - operate(pad_sides(field), operator)
    coarse = vcycle(operators, level + 1, None, restrict(residual))
    field = field + prolong(coarse)
    return field + omega_weight * (rhs - operate(pad_sides(field), operator)) / operator[0]


def reference(temp_old, virgin, zone, zone_props, gas_flux, gas_owner, gas_cell):
    squared = temp_old * temp_old
    heat_factor = 0.5 + squared
    char_blend = 0.4 + 0.6 * virgin
    props = zone_props[:, zone]
    cond_z = props[0] * heat_factor * char_blend
    cond_x = props[1] * heat_factor * char_blend
    cond_y = props[2] * heat_factor * char_blend
    rate = 8.0 * virgin * jnp.exp(-3.0 / temp_old)
    diagonal = props[3] * (0.5 + virgin) + 6.0 * rate / squared
    target = (gas_owner[:, 0] * CX + gas_cell).astype(jnp.int32)
    wall = jax.ops.segment_sum(gas_flux.astype(jnp.float32), target, num_segments=CX * N_SURF)
    source = (-2.0 * rate).at[0].add(wall)
    fields = (diagonal, cond_z, cond_x, cond_y)
    operators = []
    for level in range(LEVELS):
        level_diag, level_z, level_x, level_y = fields
        padded_z = jnp.pad(level_z, ((1, 1), (0, 0), (0, 0)))
        padded_x = jnp.pad(level_x, ((0, 0), (1, 1), (0, 0)))
        weights = weights_from_padded(padded_z, padded_x, level_y, 0.25 ** level)
        operators.append(build_operator(level_diag, weights))
        if level < LEVELS - 1:
            fields = tuple(restrict(member) for member in fields)
    solution = None
    for cycle_index in range(CYCLES):
        solution = vcycle(operators, 0, solution, source)
    return solution
```

```python
import functools

import jax
import jax.numpy as jnp
from jax import lax
from jax.experimental import pallas as pl
from jax.experimental.pallas import tpu as pltpu
from jax.sharding import PartitionSpec as P

MESH = pl.DeviceIdType.MESH
F32 = jnp.float32
OMEGA = 0.8
LANES = 128
GROUP = 16


def roll(value, shift, axis):
    return pltpu.roll(value, shift % value.shape[axis], axis)


def gas_kernel(groups, width, span, flux_ref, target_ref, wall_ref,
               flux_all, target_all, partial, parts, send1, recv1, send2, recv2):
    surf, depth = lax.axis_index("surf"), lax.axis_index("depth")
    group, member = surf // span, lax.rem(surf, span)
    collects = (depth < 2) & (lax.rem(group, 2) == depth)
    owner = depth == 0
    halo = width // 2
    window = width + 2 * halo

    def source(other):
        return (other * span + member, depth)

    def summer(other):
        return (group * span + other, lax.rem(group, 2))

    def is_self(other):
        return owner & (lax.rem(group, 2) == 0) & (other == member)

    barrier = pltpu.get_barrier_semaphore()

    @pl.when(collects)
    def _():
        def greet(other, carry):
            @pl.when(other != group)
            def _():
                pl.semaphore_signal(barrier, inc=1, device_id=source(other), device_id_type=MESH)
            return carry
        lax.fori_loop(0, groups, greet, 0)

    @pl.when(owner)
    def _():
        def greet(other, carry):
            @pl.when(jnp.logical_not(is_self(other)))
            def _():
                pl.semaphore_signal(barrier, inc=1, device_id=summer(other), device_id_type=MESH)
            return carry
        lax.fori_loop(0, span, greet, 0)

    @pl.when(depth < 2)
    def _():
        pl.semaphore_wait(barrier, groups // 2 - jnp.where(collects, 1, 0)
                          + jnp.where(collects, span - jnp.where(depth == 0, 1, 0), 0))

    def copies1(to_group, slot):
        where = (to_group * span + member, depth)
        return (
            pltpu.make_async_remote_copy(
                src_ref=flux_ref, dst_ref=flux_all.at[slot], send_sem=send1.at[0, to_group],
                recv_sem=recv1.at[0, slot], device_id=where, device_id_type=MESH),
            pltpu.make_async_remote_copy(
                src_ref=target_ref, dst_ref=target_all.at[slot], send_sem=send1.at[1, to_group],
                recv_sem=recv1.at[1, slot], device_id=where, device_id_type=MESH),
        )

    def copy2(to_member, slot):
        return pltpu.make_async_remote_copy(
            src_ref=partial.at[pl.ds(pl.multiple_of(to_member * width, 8), window)],
            dst_ref=parts.at[slot], send_sem=send2.at[to_member], recv_sem=recv2.at[slot],
            device_id=(group * span + to_member, 0), device_id_type=MESH)

    @pl.when(depth < 2)
    def _():
        def push(half, carry):
            to_group = 2 * half + depth
            @pl.when(to_group != group)
            def _():
                for copy in copies1(to_group, group):
                    copy.start()
            return carry
        lax.fori_loop(0, groups // 2, push, 0)

    @pl.when(collects)
    def _():
        flux_all[group] = flux_ref[...]
        target_all[group] = target_ref[...]
        partial[...] = jnp.zeros_like(partial)
        rows = partial.shape[0]
        ids = group * (span * width) - halo + lax.broadcasted_iota(jnp.int32, (rows, LANES), 0)

        def add(other, carry):
            @pl.when(other != group)
            def _():
                for copy in copies1(other, other):
                    copy.wait_recv()
            placing = jnp.where(ids == target_all[other], 1.0, 0.0).astype(jnp.bfloat16)
            partial[...] += jnp.dot(placing, flux_all[other], preferred_element_type=F32)
            return carry
        lax.fori_loop(0, groups, add, 0)

        def push(to_member, carry):
            itself = is_self(to_member)
            @pl.when(itself)
            def _():
                parts[member] = partial[pl.ds(pl.multiple_of(member * width, 8), window)]
            @pl.when(jnp.logical_not(itself))
            def _():
                copy2(to_member, member).start()
            return carry
        lax.fori_loop(0, span, push, 0)

    wall_ref[...] = jnp.zeros_like(wall_ref)

    @pl.when(owner)
    def _():
        def add(other, carry):
            @pl.when(jnp.logical_not(is_self(other)))
            def _():
                copy2(other, other).wait_recv()
            wall_ref[...] += parts[other]
            return carry
        lax.fori_loop(0, span, add, 0)

    @pl.when(depth < 2)
    def _():
        def drain(half, carry):
            to_group = 2 * half + depth
            @pl.when(to_group != group)
            def _():
                for copy in copies1(to_group, group):
                    copy.wait_send()
            return carry
        lax.fori_loop(0, groups // 2, drain, 0)

    @pl.when(collects)
    def _():
        def drain(to_member, carry):
            @pl.when(jnp.logical_not(is_self(to_member)))
            def _():
                copy2(to_member, member).wait_send()
            return carry
        lax.fori_loop(0, span, drain, 0)


SIDES = [(dz, dx) for dz in (-1, 0, 1) for dx in (-1, 0, 1) if (dz, dx) != (0, 0)]


class Level:
    def __init__(self, refs, halo_z, halo_x):
        self.C, self.WX, self.WY, self.WI, self.B, self.WZ, self.U = refs
        self.rows, self.cols = self.C.shape[0], self.C.shape[1]
        self.halo_z, self.halo_x = halo_z, halo_x


def residual(level, field, first, count):
    here, up, down = (pl.ds(first + shift, count) for shift in (1, 2, 0))
    own = pl.ds(first, count)
    mid = field[here]
    wx, wy = level.WX[own], level.WY[own]
    total = level.B[own] - level.C[own] * mid
    total = total + level.WZ[here] * field[up] + level.WZ[down] * field[down]
    total = total + wx * roll(mid, -1, 1) + roll(wx * mid, 1, 1)
    return total + wy * roll(mid, -1, 2) + roll(wy * mid, 1, 2)


def restrict_into(source, skip, scratch, target, target_skip):
    rows, cols = scratch.shape[0], scratch.shape[1]
    for row in range(rows):
        scratch[row] = source[skip + 2 * row] + source[skip + 2 * row + 1]
    even = scratch[:, pl.ds(0, cols // 2, stride=2), :]
    odd = scratch[:, pl.ds(1, cols // 2, stride=2), :]
    target[pl.ds(target_skip, rows)] = 0.25 * (even + odd)


def prolong_onto(level, coarse, scratch, first, count):
    cols = scratch.shape[1]
    low, number = first // 2, count // 2
    part = coarse[pl.ds(low, number)]
    scratch[pl.ds(low, number), pl.ds(0, cols // 2, stride=2), :] = part
    scratch[pl.ds(low, number), pl.ds(1, cols // 2, stride=2), :] = part
    for row in range(low, low + number):
        wide = scratch[row]
        level.U[1 + 2 * row] = level.U[1 + 2 * row] + wide
        level.U[2 + 2 * row] = level.U[2 + 2 * row] + wide


def cycles_kernel(n_surf, n_depth, n_zones,
                  temp_ref, virgin_ref, zone_ref, props_ref, wall_ref, out_ref,
                  packed, guess, temp, virgin,
                  fd0, fx0, fy0, fz0, fd1, fx1, fy1, fz1, fd2, fx2, fy2, fz2, fd3, fx3, fy3, fz3,
                  l0, l1, l2, res, t0, t1, t2, v1, v2, b3,
                  coef_own, coef_all, rhs_own, rhs_all, ratio, inverse, solved, e2,
                  z_out, z_in, x_out, x_in,
                  s_send, s_recv, e_send, e_recv, g_send, g_recv, h_send, h_recv):
    surf, depth = lax.axis_index("surf"), lax.axis_index("depth")

    def at(dz, dx):
        return (lax.rem(surf + dx + n_surf, n_surf), lax.rem(depth + dz + n_depth, n_depth))

    levels = [Level(refs, 8 >> index, 8 >> index) for index, refs in enumerate((l0, l1, l2))]
    top, mid, low = levels

    barrier = pltpu.get_barrier_semaphore()

    def greet(dz, carry):
        for dx in (-1, 0, 1):
            pl.semaphore_signal(barrier, inc=1, device_id=at(dz, dx), device_id_type=MESH)
        return carry

    for dx in (-1, 1):
        pl.semaphore_signal(barrier, inc=1, device_id=at(0, dx), device_id_type=MESH)
    lax.fori_loop(1, n_depth, greet, 0)

    own_t = temp_ref[...]
    own_v = virgin_ref[...]
    code_t = ((own_t - 0.5) * (65535.0 / 1.5) + 0.5).astype(jnp.int32)
    code_v = ((own_v - 0.2) * (65535.0 / 0.8) + 0.5).astype(jnp.int32)
    packed[1, 0:8, 8:24] = jnp.left_shift(code_t, 16) | code_v
    packed[1, 8, 8:24] = zone_ref[0]
    pl.semaphore_wait(barrier, 3 * n_depth - 1)

    src_x = {-1: (8, 8), 0: (8, 16), 1: (16, 8)}
    dst_x = {-1: 24, 0: 8, 1: 0}

    def ring_copy(index, ref_src, ref_dst, send, recv, dz, dx):
        return pltpu.make_async_remote_copy(
            src_ref=ref_src, dst_ref=ref_dst, send_sem=send.at[index], recv_sem=recv.at[index],
            device_id=at(dz, dx), device_id_type=MESH)

    def setup_copy(index):
        dz, dx = SIDES[index]
        first, count = src_x[dx]
        return ring_copy(
            index, packed.at[1, :, pl.ds(first, count)],
            packed.at[1 - dz, :, pl.ds(dst_x[dx], count)], s_send, s_recv, dz, dx)

    def guess_copy(index):
        dz, dx = SIDES[index]
        first, count = src_x[dx]
        low_row, rows = (0, 8) if dx == 0 or dz == 0 else ((0, 7) if dz < 0 else (1, 7))
        return ring_copy(
            index, guess.at[pl.ds(9 + low_row, rows), pl.ds(first, count)],
            guess.at[pl.ds(1 + 8 * (1 - dz) + low_row, rows), pl.ds(dst_x[dx], count)],
            e_send, e_recv, dz, dx)

    for index in range(8):
        setup_copy(index).start()

    def column_mask(level):
        column = lax.broadcasted_iota(jnp.int32, (level.cols, LANES), 0)
        first, last = level.halo_x, level.cols - level.halo_x
        inside = ((column >= first) | (surf > 0)) & ((column < last) | (surf < n_surf - 1))
        return jnp.where(inside, 1.0, 0.0)

    row_mask = [jnp.where(depth > 0, 1.0, 0.0), jnp.float32(1.0), jnp.where(depth < n_depth - 1, 1.0, 0.0)]
    masks = [column_mask(level) for level in levels]
    for level in levels:
        zero = jnp.zeros((level.cols, LANES), F32)
        level.WZ[0] = zero
        level.U[0] = zero
        level.U[level.rows + 1] = zero
    for ref in (fz0, fz1, fz2):
        ref[0] = jnp.zeros(ref.shape[1:], F32)
        ref[ref.shape[0] - 1] = jnp.zeros(ref.shape[1:], F32)
    guess[0] = jnp.zeros(guess.shape[1:], F32)
    guess[25] = jnp.zeros(guess.shape[1:], F32)
    solved[0] = jnp.zeros(solved.shape[1:], F32)
    solved[n_depth + 1] = jnp.zeros(solved.shape[1:], F32)

    for index in range(8):
        setup_copy(index).wait_recv()
    for block in range(3):
        code = packed[block, 0:8]
        rows = pl.ds(8 * block, 8)
        temp[rows] = 0.5 + lax.shift_right_logical(code, 16).astype(F32) * (1.5 / 65535.0)
        virgin[rows] = 0.2 + (code & 0xFFFF).astype(F32) * (0.8 / 65535.0)
    temp[8:16, 8:24] = own_t
    virgin[8:16, 8:24] = own_v
    for block in range(3):
        zone = packed[block, 8]
        inside = masks[0] * row_mask[block]
        props = [jnp.zeros((top.cols, LANES), F32) for _ in range(4)]
        for number in range(n_zones):
            hit = zone == number
            props = [jnp.where(hit, props_ref[kind, number], props[kind]) for kind in range(4)]
        props = [value * inside for value in props]
        for row in range(8 * block, 8 * block + 8, 2):
            rows = pl.ds(row, 2)
            t, v = temp[rows], virgin[rows]
            squared = t * t
            blend = (0.5 + squared) * (0.4 + 0.6 * v)
            rate = 8.0 * v * jnp.exp(-3.0 / t)
            fz0[pl.ds(row + 1, 2)] = props[0] * blend
            fx0[rows] = props[1] * blend
            fy0[rows] = props[2] * blend
            fd0[rows] = (props[3] * (0.5 + v) + 6.0 * rate / squared) * inside
            top.B[rows] = -2.0 * rate * inside

    fields = [(fd0, fx0, fy0, fz0), (fd1, fx1, fy1, fz1), (fd2, fx2, fy2, fz2), (fd3, fx3, fy3, fz3)]
    scratches = (t0, t1, t2)

    for index, level in enumerate(levels):
        fd, fx, fy, fz = fields[index]
        half = 0.5 * 0.25**index
        step = min(4, level.halo_z)
        lane = lax.broadcasted_iota(jnp.int32, (step, level.cols, LANES), 2)
        for row in range(0, level.rows, step):
            rows = pl.ds(row, step)
            inside = masks[index] * row_mask[row // level.halo_z]
            here = fz[pl.ds(row + 1, step)]
            lower = half * (here + fz[rows])
            upper = half * (here + fz[pl.ds(row + 2, step)])
            level.WZ[pl.ds(row + 1, step)] = upper
            across = fx[rows]
            east = half * (across + roll(across, -1, 1))
            west = roll(east, 1, 1)
            level.WX[rows] = east
            along = fy[rows]
            north = 0.5 * (along + jnp.where(lane == LANES - 1, 0.0, roll(along, -1, 2)))
            south = 0.5 * (along + jnp.where(lane == 0, 0.0, roll(along, 1, 2)))
            level.WY[rows] = jnp.where(lane == LANES - 1, 0.0, north)
            centre = fd[rows] + lower + upper + west + east + south + north
            level.C[rows] = centre
            level.WI[rows] = jnp.where((inside > 0.0)[None], OMEGA / centre, 0.0)
        for kind in range(4):
            skip = 1 if kind == 3 else 0
            target_skip = 1 if kind == 3 and index < 2 else 0
            restrict_into(fields[index][kind], skip, scratches[index], fields[index + 1][kind], target_skip)

    half = 0.5 * 0.25**3
    centre_z, centre_x, centre_y = fz3[1, 1:3], fx3[1, 1:3], fy3[1, 1:3]
    lane = lax.broadcasted_iota(jnp.int32, (2, LANES), 1)
    lower = half * (centre_z + fz3[0, 1:3])
    upper = half * (centre_z + fz3[2, 1:3])
    west = half * (centre_x + fx3[1, 0:2])
    east = half * (centre_x + fx3[1, 2:4])
    north = 0.5 * (centre_y + jnp.where(lane == LANES - 1, 0.0, roll(centre_y, -1, 1)))
    south = 0.5 * (centre_y + jnp.where(lane == 0, 0.0, roll(centre_y, 1, 1)))
    centre = fd3[1, 1:3] + lower + upper + west + east + south + north
    for column in range(2):
        coef_own[0, column] = centre[column : column + 1]
        coef_own[1, column] = upper[column : column + 1]

    source_column = {-1: (0, 1), 0: (0, 2), 1: (1, 1)}
    landing_column = {-1: 3, 0: 1, 1: 0}

    def column_copy(phase, dz, dx):
        first, count = source_column[dx]
        if phase == 0:
            src, dst = coef_own.at[:, pl.ds(first, count)], coef_all.at[depth, :, pl.ds(landing_column[dx], count)]
        else:
            src = rhs_own.at[phase - 1, pl.ds(first, count)]
            dst = rhs_all.at[phase - 1, depth, pl.ds(landing_column[dx], count)]
        return pltpu.make_async_remote_copy(
            src_ref=src, dst_ref=dst, send_sem=g_send.at[phase, dz, dx + 1],
            recv_sem=g_recv.at[phase, dz, dx + 1], device_id=at(dz, dx), device_id_type=MESH)

    def each_column(phase, act):
        for dx in (-1, 1):
            act(column_copy(phase, 0, dx))

        def body(dz, carry):
            for dx in (-1, 0, 1):
                act(column_copy(phase, dz, dx))
            return carry

        lax.fori_loop(1, n_depth, body, 0)

    each_column(0, lambda copy: copy.start())
    coef_all[depth, :, 1:3] = coef_own[...]

    @pl.when(depth == 0)
    def _():
        top.B[8] = top.B[8] + wall_ref[...]

    def down(level, scratch, coarse_rhs, chunk):
        for row in range(0, level.rows, chunk):
            res[pl.ds(row, chunk), 0 : level.cols] = residual(level, level.U, row, chunk)
        restrict_into(res.at[:, pl.ds(0, level.cols)], 0, scratch, coarse_rhs, 0)

    def near_copies(cycle):
        pairs = []
        for index, (dz, dx) in enumerate(((-1, 0), (1, 0), (0, -1), (0, 1))):
            side = index % 2
            out, into = (z_out, z_in) if dz else (x_out, x_in)
            pairs.append(pltpu.make_async_remote_copy(
                src_ref=out.at[cycle, side], dst_ref=into.at[cycle, 1 - side],
                send_sem=h_send.at[cycle, index], recv_sem=h_recv.at[cycle, index],
                device_id=at(dz, dx), device_id_type=MESH))
        return pairs

    def run_cycle(cycle, last):
        down(top, t0, mid.B, 4)
        mid.U[1:13] = mid.WI[...] * mid.B[...]
        down(mid, t1, low.B, 4)
        low.U[1:7] = low.WI[...] * low.B[...]
        down(low, t2, b3, 6)
        for column in range(2):
            rhs_own[cycle, column] = b3[1, 1 + column : 2 + column]
        each_column(1 + cycle, lambda copy: copy.start())
        z_out[cycle, 0, 0] = low.B[2]
        z_out[cycle, 0, 1] = low.U[4]
        z_out[cycle, 1, 0] = low.B[3]
        z_out[cycle, 1, 1] = low.U[3]
        for row in range(4):
            x_out[cycle, 0, row] = low.U[2 + row, 3:4]
            x_out[cycle, 1, row] = low.U[2 + row, 4:5]
        near = near_copies(cycle)
        for copy in near:
            copy.start()
        rhs_all[cycle, depth, 1:3] = rhs_own[cycle]

        if cycle == 0:
            each_column(0, lambda copy: copy.wait_recv())
            inv = 1.0 / coef_all[0, 0]
            inverse[0] = inv
            ratio[0] = coef_all[0, 1] * inv
            for row in range(1, n_depth):
                inv = 1.0 / (coef_all[row, 0] - coef_all[row - 1, 1] * ratio[row - 1])
                inverse[row] = inv
                ratio[row] = coef_all[row, 1] * inv

        for copy in near:
            copy.wait_recv()
        low.B[1] = z_in[cycle, 0, 0]
        low.B[4] = z_in[cycle, 1, 0]
        low.U[2] = low.WI[1] * low.B[1]
        low.U[5] = low.WI[4] * low.B[4]
        low.U[1] = z_in[cycle, 0, 1] * (masks[2] * row_mask[0])
        low.U[6] = z_in[cycle, 1, 1] * (masks[2] * row_mask[2])
        for row in range(4):
            block = (0, 1, 1, 2)[row]
            first = jnp.where(surf > 0, 1.0, 0.0) * row_mask[block]
            final = jnp.where(surf < n_surf - 1, 1.0, 0.0) * row_mask[block]
            low.U[2 + row, 0:1] = x_in[cycle, 0, row] * first
            low.U[2 + row, 7:8] = x_in[cycle, 1, row] * final

        each_column(1 + cycle, lambda copy: copy.wait_recv())
        value = rhs_all[cycle, 0] * inverse[0]
        values = [value]
        for row in range(1, n_depth):
            value = (rhs_all[cycle, row] + coef_all[row - 1, 1] * value) * inverse[row]
            values.append(value)
        later = values[-1]
        solved[n_depth] = later
        for row in range(n_depth - 2, -1, -1):
            later = values[row] + ratio[row] * later
            solved[row + 1] = later
        for row in range(3):
            for column in range(4):
                value = solved[depth + row, column]
                if column == 0:
                    value = value * jnp.where(surf > 0, 1.0, 0.0)
                if column == 3:
                    value = value * jnp.where(surf < n_surf - 1, 1.0, 0.0)
                e2[row, 2 * column : 2 * column + 2] = jnp.broadcast_to(value, (2, LANES))
        for row in range(3):
            wide = e2[row]
            low.U[1 + 2 * row] = low.U[1 + 2 * row] + wide
            low.U[2 + 2 * row] = low.U[2 + 2 * row] + wide
        v2[...] = low.U[1:7] + low.WI[...] * residual(low, low.U, 0, 6)
        prolong_onto(mid, v2, t1, 2, 8)
        v1[2:10] = mid.U[3:11] + mid.WI[2:10] * residual(mid, mid.U, 2, 8)
        prolong_onto(top, v1, t0, 6, 12)
        for row in range(8, 16, 4):
            rows = pl.ds(row, 4)
            new = top.U[pl.ds(row + 1, 4)] + top.WI[rows] * residual(top, top.U, row, 4)
            if last:
                out_ref[pl.ds(row - 8, 4)] = new[:, 8:24]
            else:
                guess[pl.ds(row + 1, 4), 8:24] = new[:, 8:24]

    top.U[1:25] = top.WI[...] * top.B[...]
    run_cycle(0, False)
    for index in range(8):
        guess_copy(index).start()
    for index in range(8):
        guess_copy(index).wait_recv()
    for rows in (pl.ds(1, 1), pl.ds(24, 1)):
        for columns in (pl.ds(0, 8), pl.ds(24, 8)):
            guess[rows, columns] = jnp.zeros((1, 8, LANES), F32)
    for block in range(3):
        rows = pl.ds(1 + 8 * block, 8)
        if block == 1:
            for columns, inside in ((slice(0, 8), surf > 0), (slice(24, 32), surf < n_surf - 1)):
                guess[rows, columns] = guess[rows, columns] * jnp.where(inside, 1.0, 0.0)
        else:
            guess[rows] = guess[rows] * (masks[0] * row_mask[block])
    for row in range(0, 24, 4):
        rows, padded = pl.ds(row, 4), pl.ds(row + 1, 4)
        top.U[padded] = guess[padded] + top.WI[rows] * residual(top, guess, row, 4)
    run_cycle(1, True)

    for index in range(8):
        setup_copy(index).wait_send()
        guess_copy(index).wait_send()
    for phase in range(3):
        each_column(phase, lambda copy: copy.wait_send())
    for cycle in range(2):
        for copy in near_copies(cycle):
            copy.wait_send()


def per_device(n_surf, n_depth, temp_old, virgin, zone, zone_props, gas_flux, gas_owner, gas_cell):
    width = temp_old.shape[1]
    span = min(GROUP, n_surf // 2)
    groups = n_surf // span
    vmem = pl.BlockSpec(memory_space=pltpu.VMEM)
    smem = pl.BlockSpec(memory_space=pltpu.SMEM)
    dma = pltpu.SemaphoreType.DMA
    rows = gas_flux.shape[0]
    target = (gas_owner[:, 0] * width + gas_cell).reshape(1, rows)

    wall = pl.pallas_call(
        functools.partial(gas_kernel, groups, width, span),
        out_shape=jax.ShapeDtypeStruct((2 * width, LANES), F32),
        in_specs=[vmem, vmem],
        out_specs=vmem,
        scratch_shapes=[
            pltpu.VMEM((groups, rows, LANES), jnp.bfloat16),
            pltpu.VMEM((groups, 1, rows), jnp.int32),
            pltpu.VMEM((span * width + width, LANES), F32),
            pltpu.VMEM((span, 2 * width, LANES), F32),
            dma((2, groups)), dma((2, groups)), dma((span,)), dma((span,)),
        ],
        compiler_params=pltpu.CompilerParams(collective_id=0, has_side_effects=True),
        name="wall",
    )(gas_flux, target)

    def box(*shape):
        return pltpu.VMEM((*shape, LANES), F32)

    def fields(index):
        r, c = 24 >> index, 32 >> index
        return [box(r, c), box(r, c), box(r, c), box(r if index == 3 else r + 2, c)]

    def level(index):
        r, c = 24 >> index, 32 >> index
        return [box(r, c)] * 5 + [box(r + 2, c)] * 2

    scratch = [
        pltpu.VMEM((3, 9, 32, LANES), jnp.int32), box(26, 32), box(24, 32), box(24, 32),
        *fields(0), *fields(1), *fields(2), *fields(3),
        level(0), level(1), level(2),
        box(24, 32), box(12, 32), box(6, 16), box(3, 8), box(12, 16), box(6, 8), box(3, 4),
        box(2, 2, 1), box(n_depth, 2, 4, 1), box(2, 2, 1), box(2, n_depth, 4, 1),
        box(n_depth, 4, 1), box(n_depth, 4, 1), box(n_depth + 2, 4, 1), box(3, 8),
        box(2, 2, 2, 8), box(2, 2, 2, 8), box(2, 2, 4, 1), box(2, 2, 4, 1),
        dma((8,)), dma((8,)), dma((8,)), dma((8,)),
        dma((3, n_depth, 3)), dma((3, n_depth, 3)), dma((2, 4)), dma((2, 4)),
    ]
    return pl.pallas_call(
        functools.partial(cycles_kernel, n_surf, n_depth, zone_props.shape[1]),
        out_shape=jax.ShapeDtypeStruct(temp_old.shape, F32),
        in_specs=[vmem, vmem, vmem, smem, vmem],
        out_specs=vmem,
        scratch_shapes=scratch,
        compiler_params=pltpu.CompilerParams(
            collective_id=1, has_side_effects=True, vmem_limit_bytes=48 * 1024 * 1024),
        name="cycles",
    )(temp_old, virgin, zone, zone_props, wall)


def solution(mesh):
    return jax.shard_map(
        functools.partial(per_device, mesh.shape["surf"], mesh.shape["depth"]),
        mesh=mesh,
        in_specs=(
            P("depth", "surf", None),
            P("depth", "surf", None),
            P("depth", "surf", None),
            P(),
            P("surf", None),
            P("surf", None),
            P("surf"),
        ),
        out_specs=P("depth", "surf", None),
        check_vma=False,
    )
```

```python
import functools

import jax
import jax.numpy as jnp
from jax import lax
from jax.experimental import pallas as pl
from jax.experimental.pallas import tpu as pltpu
from jax.sharding import PartitionSpec as P

MESH = pl.DeviceIdType.MESH
F32 = jnp.float32
OMEGA = 0.8
LANES = 128
GROUP = 16


def roll(value, shift, axis):
    return pltpu.roll(value, shift % value.shape[axis], axis)


class Wall:
    def __init__(self, groups, span, width, refs):
        (self.flux, self.target, self.flux_all, self.target_all, self.partial, self.parts,
         self.send1, self.recv1, self.send2, self.recv2) = refs
        self.groups, self.span, self.width = groups, span, width
        surf, self.depth = lax.axis_index("surf"), lax.axis_index("depth")
        self.group, self.member = surf // span, lax.rem(surf, span)
        self.collects = (self.depth < 2) & (lax.rem(self.group, 2) == self.depth)
        self.owner = self.depth == 0

    def is_self(self, other):
        return self.owner & (lax.rem(self.group, 2) == 0) & (other == self.member)

    def copies1(self, to_group, slot):
        where = (to_group * self.span + self.member, self.depth)
        return [
            pltpu.make_async_remote_copy(
                src_ref=src, dst_ref=dst.at[slot], send_sem=self.send1.at[kind, to_group],
                recv_sem=self.recv1.at[kind, slot], device_id=where, device_id_type=MESH)
            for kind, (src, dst) in enumerate(((self.flux, self.flux_all), (self.target, self.target_all)))
        ]

    def rows_for(self, member):
        return self.partial.at[pl.ds(pl.multiple_of(member * self.width, 8), 2 * self.width)]

    def copy2(self, to_member, slot):
        return pltpu.make_async_remote_copy(
            src_ref=self.rows_for(to_member), dst_ref=self.parts.at[slot],
            send_sem=self.send2.at[to_member], recv_sem=self.recv2.at[slot],
            device_id=(self.group * self.span + to_member, 0), device_id_type=MESH)

    def greet(self, barrier):
        @pl.when(self.collects)
        def _():
            def body(other, carry):
                @pl.when(other != self.group)
                def _():
                    pl.semaphore_signal(
                        barrier, inc=1, device_id=(other * self.span + self.member, self.depth), device_id_type=MESH)
                return carry
            lax.fori_loop(0, self.groups, body, 0)

        @pl.when(self.owner)
        def _():
            def body(other, carry):
                @pl.when(jnp.logical_not(self.is_self(other)))
                def _():
                    pl.semaphore_signal(
                        barrier, inc=1, device_id=(self.group * self.span + other, lax.rem(self.group, 2)),
                        device_id_type=MESH)
                return carry
            lax.fori_loop(0, self.span, body, 0)

    def greetings(self):
        collecting = jnp.where(self.collects, 1, 0)
        from_owners = collecting * (self.span - jnp.where(self.owner, 1, 0))
        return jnp.where(self.depth < 2, self.groups // 2 - collecting, 0) + from_owners

    def each_group(self, act):
        @pl.when(self.depth < 2)
        def _():
            def body(half, carry):
                to_group = 2 * half + self.depth
                @pl.when(to_group != self.group)
                def _():
                    for copy in self.copies1(to_group, self.group):
                        act(copy)
                return carry
            lax.fori_loop(0, self.groups // 2, body, 0)

    def each_member(self, act):
        def body(member, carry):
            @pl.when(jnp.logical_not(self.is_self(member)))
            def _():
                act(self.copy2(member, self.member))
            return carry
        lax.fori_loop(0, self.span, body, 0)

    def collect(self):
        @pl.when(self.collects)
        def _():
            self.flux_all[self.group] = self.flux[...]
            self.target_all[self.group] = self.target[...]
            self.partial[...] = jnp.zeros_like(self.partial)
            rows = self.partial.shape[0]
            first = self.group * (self.span * self.width) - self.width // 2
            ids = first + lax.broadcasted_iota(jnp.int32, (rows, LANES), 0)

            def add(other, carry):
                @pl.when(other != self.group)
                def _():
                    for copy in self.copies1(other, other):
                        copy.wait_recv()
                placing = jnp.where(ids == self.target_all[other], 1.0, 0.0).astype(jnp.bfloat16)
                self.partial[...] += jnp.dot(placing, self.flux_all[other], preferred_element_type=F32)
                return carry
            lax.fori_loop(0, self.groups, add, 0)

            @pl.when(self.is_self(self.member))
            def _():
                self.parts[self.member] = self.rows_for(self.member)[...]
            self.each_member(lambda copy: copy.start())

    def add_to(self, source, row):
        @pl.when(self.owner)
        def _():
            def body(other, carry):
                @pl.when(jnp.logical_not(self.is_self(other)))
                def _():
                    self.copy2(other, other).wait_recv()
                source[row] = source[row] + self.parts[other]
                return carry
            lax.fori_loop(0, self.span, body, 0)

    def finish(self):
        self.each_group(lambda copy: copy.wait_send())

        @pl.when(self.collects)
        def _():
            self.each_member(lambda copy: copy.wait_send())


SIDES = [(dz, dx) for dz in (-1, 0, 1) for dx in (-1, 0, 1) if (dz, dx) != (0, 0)]


class Level:
    def __init__(self, refs, halo_z, halo_x):
        self.C, self.WX, self.WY, self.WI, self.B, self.WZ, self.U = refs
        self.rows, self.cols = self.C.shape[0], self.C.shape[1]
        self.halo_z, self.halo_x = halo_z, halo_x


def residual(level, field, first, count):
    here, up, down = (pl.ds(first + shift, count) for shift in (1, 2, 0))
    own = pl.ds(first, count)
    mid = field[here]
    wx, wy = level.WX[own], level.WY[own]
    total = level.B[own] - level.C[own] * mid
    total = total + level.WZ[here] * field[up] + level.WZ[down] * field[down]
    total = total + wx * roll(mid, -1, 1) + roll(wx * mid, 1, 1)
    return total + wy * roll(mid, -1, 2) + roll(wy * mid, 1, 2)


def restrict_into(source, skip, scratch, target, target_skip):
    rows, cols = scratch.shape[0], scratch.shape[1]
    for row in range(rows):
        scratch[row] = source[skip + 2 * row] + source[skip + 2 * row + 1]
    even = scratch[:, pl.ds(0, cols // 2, stride=2), :]
    odd = scratch[:, pl.ds(1, cols // 2, stride=2), :]
    target[pl.ds(target_skip, rows)] = 0.25 * (even + odd)


def prolong_onto(level, coarse, scratch, first, count):
    cols = scratch.shape[1]
    low, number = first // 2, count // 2
    part = coarse[pl.ds(low, number)]
    scratch[pl.ds(low, number), pl.ds(0, cols // 2, stride=2), :] = part
    scratch[pl.ds(low, number), pl.ds(1, cols // 2, stride=2), :] = part
    for row in range(low, low + number):
        wide = scratch[row]
        level.U[1 + 2 * row] = level.U[1 + 2 * row] + wide
        level.U[2 + 2 * row] = level.U[2 + 2 * row] + wide


def cycles_kernel(n_surf, n_depth, n_zones, groups, span,
                  temp_hbm, virgin_hbm, zone_hbm, props_hbm, flux_hbm, owner_hbm, cell_hbm, out_ref,
                  temp_ref, virgin_ref, zone_ref, props_ref, owner_ref, cell_ref, in_sem, wall_refs,
                  packed, guess, temp, virgin,
                  fd0, fx0, fy0, fz0, fd1, fx1, fy1, fz1, fd2, fx2, fy2, fz2, fd3, fx3, fy3, fz3,
                  l0, l1, l2, res, t0, t1, t2, v1, v2, b3,
                  coef_own, coef_all, rhs_own, rhs_all, ratio, inverse, solved, e2,
                  z_out, z_in, x_out, x_in,
                  s_send, s_recv, e_send, e_recv, g_send, g_recv, h_send, h_recv):
    surf, depth = lax.axis_index("surf"), lax.axis_index("depth")

    def at(dz, dx):
        return (lax.rem(surf + dx + n_surf, n_surf), lax.rem(depth + dz + n_depth, n_depth))

    levels = [Level(refs, 8 >> index, 8 >> index) for index, refs in enumerate((l0, l1, l2))]
    top, mid, low = levels

    width = out_ref.shape[1]
    wall = Wall(groups, span, width, wall_refs)
    inputs = [
        pltpu.make_async_copy(src, dst, in_sem.at[index])
        for index, (src, dst) in enumerate((
            (temp_hbm, temp_ref), (virgin_hbm, virgin_ref), (zone_hbm.at[0], zone_ref), (flux_hbm, wall.flux),
            (owner_hbm, owner_ref), (cell_hbm, cell_ref), (props_hbm, props_ref)))
    ]
    for copy in inputs:
        copy.start()

    barrier = pltpu.get_barrier_semaphore()

    def greet(dz, carry):
        for dx in (-1, 0, 1):
            pl.semaphore_signal(barrier, inc=1, device_id=at(dz, dx), device_id_type=MESH)
        return carry

    for dx in (-1, 1):
        pl.semaphore_signal(barrier, inc=1, device_id=at(0, dx), device_id_type=MESH)
    lax.fori_loop(1, n_depth, greet, 0)
    wall.greet(barrier)
    for copy in inputs:
        copy.wait()
    wall.target[...] = owner_ref[...] * width + cell_ref[...]

    own_t = temp_ref[...]
    own_v = virgin_ref[...]
    code_t = ((own_t - 0.5) * (65535.0 / 1.5) + 0.5).astype(jnp.int32)
    code_v = ((own_v - 0.2) * (65535.0 / 0.8) + 0.5).astype(jnp.int32)
    packed[1, 0:8, 8:24] = jnp.left_shift(code_t, 16) | code_v
    packed[1, 8, 8:24] = zone_ref[...]
    pl.semaphore_wait(barrier, 3 * n_depth - 1 + wall.greetings())

    src_x = {-1: (8, 8), 0: (8, 16), 1: (16, 8)}
    dst_x = {-1: 24, 0: 8, 1: 0}

    def ring_copy(index, ref_src, ref_dst, send, recv, dz, dx):
        return pltpu.make_async_remote_copy(
            src_ref=ref_src, dst_ref=ref_dst, send_sem=send.at[index], recv_sem=recv.at[index],
            device_id=at(dz, dx), device_id_type=MESH)

    def setup_copy(index):
        dz, dx = SIDES[index]
        first, count = src_x[dx]
        return ring_copy(
            index, packed.at[1, :, pl.ds(first, count)],
            packed.at[1 - dz, :, pl.ds(dst_x[dx], count)], s_send, s_recv, dz, dx)

    def guess_copy(index):
        dz, dx = SIDES[index]
        first, count = src_x[dx]
        low_row, rows = (0, 8) if dx == 0 or dz == 0 else ((0, 7) if dz < 0 else (1, 7))
        return ring_copy(
            index, guess.at[pl.ds(9 + low_row, rows), pl.ds(first, count)],
            guess.at[pl.ds(1 + 8 * (1 - dz) + low_row, rows), pl.ds(dst_x[dx], count)],
            e_send, e_recv, dz, dx)

    wall.each_group(lambda copy: copy.start())
    for index in range(8):
        setup_copy(index).start()

    def column_mask(level):
        column = lax.broadcasted_iota(jnp.int32, (level.cols, LANES), 0)
        first, last = level.halo_x, level.cols - level.halo_x
        inside = ((column >= first) | (surf > 0)) & ((column < last) | (surf < n_surf - 1))
        return jnp.where(inside, 1.0, 0.0)

    row_mask = [jnp.where(depth > 0, 1.0, 0.0), jnp.float32(1.0), jnp.where(depth < n_depth - 1, 1.0, 0.0)]
    masks = [column_mask(level) for level in levels]
    for level in levels:
        zero = jnp.zeros((level.cols, LANES), F32)
        level.WZ[0] = zero
        level.U[0] = zero
        level.U[level.rows + 1] = zero
    for ref in (fz0, fz1, fz2):
        ref[0] = jnp.zeros(ref.shape[1:], F32)
        ref[ref.shape[0] - 1] = jnp.zeros(ref.shape[1:], F32)
    guess[0] = jnp.zeros(guess.shape[1:], F32)
    guess[25] = jnp.zeros(guess.shape[1:], F32)
    solved[0] = jnp.zeros(solved.shape[1:], F32)
    solved[n_depth + 1] = jnp.zeros(solved.shape[1:], F32)

    wall.collect()

    for index in range(8):
        setup_copy(index).wait_recv()
    for block in range(3):
        code = packed[block, 0:8]
        rows = pl.ds(8 * block, 8)
        temp[rows] = 0.5 + lax.shift_right_logical(code, 16).astype(F32) * (1.5 / 65535.0)
        virgin[rows] = 0.2 + (code & 0xFFFF).astype(F32) * (0.8 / 65535.0)
    temp[8:16, 8:24] = own_t
    virgin[8:16, 8:24] = own_v
    for block in range(3):
        zone = packed[block, 8]
        inside = masks[0] * row_mask[block]
        props = [jnp.zeros((top.cols, LANES), F32) for _ in range(4)]
        for number in range(n_zones):
            hit = zone == number
            props = [jnp.where(hit, props_ref[kind, number], props[kind]) for kind in range(4)]
        props = [value * inside for value in props]
        for row in range(8 * block, 8 * block + 8, 2):
            rows = pl.ds(row, 2)
            t, v = temp[rows], virgin[rows]
            squared = t * t
            blend = (0.5 + squared) * (0.4 + 0.6 * v)
            rate = 8.0 * v * jnp.exp(-3.0 / t)
            fz0[pl.ds(row + 1, 2)] = props[0] * blend
            fx0[rows] = props[1] * blend
            fy0[rows] = props[2] * blend
            fd0[rows] = (props[3] * (0.5 + v) + 6.0 * rate / squared) * inside
            top.B[rows] = -2.0 * rate * inside

    fields = [(fd0, fx0, fy0, fz0), (fd1, fx1, fy1, fz1), (fd2, fx2, fy2, fz2), (fd3, fx3, fy3, fz3)]
    scratches = (t0, t1, t2)

    for index, level in enumerate(levels):
        fd, fx, fy, fz = fields[index]
        half = 0.5 * 0.25**index
        step = min(4, level.halo_z)
        lane = lax.broadcasted_iota(jnp.int32, (step, level.cols, LANES), 2)
        for row in range(0, level.rows, step):
            rows = pl.ds(row, step)
            inside = masks[index] * row_mask[row // level.halo_z]
            here = fz[pl.ds(row + 1, step)]
            lower = half * (here + fz[rows])
            upper = half * (here + fz[pl.ds(row + 2, step)])
            level.WZ[pl.ds(row + 1, step)] = upper
            across = fx[rows]
            east = half * (across + roll(across, -1, 1))
            west = roll(east, 1, 1)
            level.WX[rows] = east
            along = fy[rows]
            north = 0.5 * (along + jnp.where(lane == LANES - 1, 0.0, roll(along, -1, 2)))
            south = 0.5 * (along + jnp.where(lane == 0, 0.0, roll(along, 1, 2)))
            level.WY[rows] = jnp.where(lane == LANES - 1, 0.0, north)
            centre = fd[rows] + lower + upper + west + east + south + north
            level.C[rows] = centre
            level.WI[rows] = jnp.where((inside > 0.0)[None], OMEGA / centre, 0.0)
        for kind in range(4):
            skip = 1 if kind == 3 else 0
            target_skip = 1 if kind == 3 and index < 2 else 0
            restrict_into(fields[index][kind], skip, scratches[index], fields[index + 1][kind], target_skip)

    half = 0.5 * 0.25**3
    centre_z, centre_x, centre_y = fz3[1, 1:3], fx3[1, 1:3], fy3[1, 1:3]
    lane = lax.broadcasted_iota(jnp.int32, (2, LANES), 1)
    lower = half * (centre_z + fz3[0, 1:3])
    upper = half * (centre_z + fz3[2, 1:3])
    west = half * (centre_x + fx3[1, 0:2])
    east = half * (centre_x + fx3[1, 2:4])
    north = 0.5 * (centre_y + jnp.where(lane == LANES - 1, 0.0, roll(centre_y, -1, 1)))
    south = 0.5 * (centre_y + jnp.where(lane == 0, 0.0, roll(centre_y, 1, 1)))
    centre = fd3[1, 1:3] + lower + upper + west + east + south + north
    for column in range(2):
        coef_own[0, column] = centre[column : column + 1]
        coef_own[1, column] = upper[column : column + 1]

    source_column = {-1: (0, 1), 0: (0, 2), 1: (1, 1)}
    landing_column = {-1: 3, 0: 1, 1: 0}

    def column_copy(phase, dz, dx):
        first, count = source_column[dx]
        if phase == 0:
            src, dst = coef_own.at[:, pl.ds(first, count)], coef_all.at[depth, :, pl.ds(landing_column[dx], count)]
        else:
            src = rhs_own.at[phase - 1, pl.ds(first, count)]
            dst = rhs_all.at[phase - 1, depth, pl.ds(landing_column[dx], count)]
        return pltpu.make_async_remote_copy(
            src_ref=src, dst_ref=dst, send_sem=g_send.at[phase, dz, dx + 1],
            recv_sem=g_recv.at[phase, dz, dx + 1], device_id=at(dz, dx), device_id_type=MESH)

    def each_column(phase, act):
        for dx in (-1, 1):
            act(column_copy(phase, 0, dx))

        def body(dz, carry):
            for dx in (-1, 0, 1):
                act(column_copy(phase, dz, dx))
            return carry

        lax.fori_loop(1, n_depth, body, 0)

    each_column(0, lambda copy: copy.start())
    coef_all[depth, :, 1:3] = coef_own[...]

    wall.add_to(top.B, 8)

    def down(level, scratch, coarse_rhs, chunk):
        for row in range(0, level.rows, chunk):
            res[pl.ds(row, chunk), 0 : level.cols] = residual(level, level.U, row, chunk)
        restrict_into(res.at[:, pl.ds(0, level.cols)], 0, scratch, coarse_rhs, 0)

    def near_copies(cycle):
        pairs = []
        for index, (dz, dx) in enumerate(((-1, 0), (1, 0), (0, -1), (0, 1))):
            side = index % 2
            out, into = (z_out, z_in) if dz else (x_out, x_in)
            pairs.append(pltpu.make_async_remote_copy(
                src_ref=out.at[cycle, side], dst_ref=into.at[cycle, 1 - side],
                send_sem=h_send.at[cycle, index], recv_sem=h_recv.at[cycle, index],
                device_id=at(dz, dx), device_id_type=MESH))
        return pairs

    def run_cycle(cycle, last):
        down(top, t0, mid.B, 4)
        mid.U[1:13] = mid.WI[...] * mid.B[...]
        down(mid, t1, low.B, 4)
        low.U[1:7] = low.WI[...] * low.B[...]
        down(low, t2, b3, 6)
        for column in range(2):
            rhs_own[cycle, column] = b3[1, 1 + column : 2 + column]
        each_column(1 + cycle, lambda copy: copy.start())
        z_out[cycle, 0, 0] = low.B[2]
        z_out[cycle, 0, 1] = low.U[4]
        z_out[cycle, 1, 0] = low.B[3]
        z_out[cycle, 1, 1] = low.U[3]
        for row in range(4):
            x_out[cycle, 0, row] = low.U[2 + row, 3:4]
            x_out[cycle, 1, row] = low.U[2 + row, 4:5]
        near = near_copies(cycle)
        for copy in near:
            copy.start()
        rhs_all[cycle, depth, 1:3] = rhs_own[cycle]

        if cycle == 0:
            each_column(0, lambda copy: copy.wait_recv())
            inv = 1.0 / coef_all[0, 0]
            inverse[0] = inv
            ratio[0] = coef_all[0, 1] * inv
            for row in range(1, n_depth):
                inv = 1.0 / (coef_all[row, 0] - coef_all[row - 1, 1] * ratio[row - 1])
                inverse[row] = inv
                ratio[row] = coef_all[row, 1] * inv

        for copy in near:
            copy.wait_recv()
        low.B[1] = z_in[cycle, 0, 0]
        low.B[4] = z_in[cycle, 1, 0]
        low.U[2] = low.WI[1] * low.B[1]
        low.U[5] = low.WI[4] * low.B[4]
        low.U[1] = z_in[cycle, 0, 1] * (masks[2] * row_mask[0])
        low.U[6] = z_in[cycle, 1, 1] * (masks[2] * row_mask[2])
        for row in range(4):
            block = (0, 1, 1, 2)[row]
            first = jnp.where(surf > 0, 1.0, 0.0) * row_mask[block]
            final = jnp.where(surf < n_surf - 1, 1.0, 0.0) * row_mask[block]
            low.U[2 + row, 0:1] = x_in[cycle, 0, row] * first
            low.U[2 + row, 7:8] = x_in[cycle, 1, row] * final

        each_column(1 + cycle, lambda copy: copy.wait_recv())
        value = rhs_all[cycle, 0] * inverse[0]
        values = [value]
        for row in range(1, n_depth):
            value = (rhs_all[cycle, row] + coef_all[row - 1, 1] * value) * inverse[row]
            values.append(value)
        later = values[-1]
        solved[n_depth] = later
        for row in range(n_depth - 2, -1, -1):
            later = values[row] + ratio[row] * later
            solved[row + 1] = later
        for row in range(3):
            for column in range(4):
                value = solved[depth + row, column]
                if column == 0:
                    value = value * jnp.where(surf > 0, 1.0, 0.0)
                if column == 3:
                    value = value * jnp.where(surf < n_surf - 1, 1.0, 0.0)
                e2[row, 2 * column : 2 * column + 2] = jnp.broadcast_to(value, (2, LANES))
        for row in range(3):
            wide = e2[row]
            low.U[1 + 2 * row] = low.U[1 + 2 * row] + wide
            low.U[2 + 2 * row] = low.U[2 + 2 * row] + wide
        v2[...] = low.U[1:7] + low.WI[...] * residual(low, low.U, 0, 6)
        prolong_onto(mid, v2, t1, 2, 8)
        v1[2:10] = mid.U[3:11] + mid.WI[2:10] * residual(mid, mid.U, 2, 8)
        prolong_onto(top, v1, t0, 6, 12)
        for row in range(8, 16, 4):
            rows = pl.ds(row, 4)
            new = top.U[pl.ds(row + 1, 4)] + top.WI[rows] * residual(top, top.U, row, 4)
            if last:
                out_ref[pl.ds(row - 8, 4)] = new[:, 8:24]
            else:
                guess[pl.ds(row + 1, 4), 8:24] = new[:, 8:24]

    top.U[1:25] = top.WI[...] * top.B[...]
    run_cycle(0, False)
    for index in range(8):
        guess_copy(index).start()
    for index in range(8):
        guess_copy(index).wait_recv()
    for rows in (pl.ds(1, 1), pl.ds(24, 1)):
        for columns in (pl.ds(0, 8), pl.ds(24, 8)):
            guess[rows, columns] = jnp.zeros((1, 8, LANES), F32)
    for block in range(3):
        rows = pl.ds(1 + 8 * block, 8)
        if block == 1:
            for columns, inside in ((slice(0, 8), surf > 0), (slice(24, 32), surf < n_surf - 1)):
                guess[rows, columns] = guess[rows, columns] * jnp.where(inside, 1.0, 0.0)
        else:
            guess[rows] = guess[rows] * (masks[0] * row_mask[block])
    for row in range(0, 24, 4):
        rows, padded = pl.ds(row, 4), pl.ds(row + 1, 4)
        top.U[padded] = guess[padded] + top.WI[rows] * residual(top, guess, row, 4)
    run_cycle(1, True)

    for index in range(8):
        setup_copy(index).wait_send()
        guess_copy(index).wait_send()
    wall.finish()
    for phase in range(3):
        each_column(phase, lambda copy: copy.wait_send())
    for cycle in range(2):
        for copy in near_copies(cycle):
            copy.wait_send()


def per_device(n_surf, n_depth, temp_old, virgin, zone, zone_props, gas_flux, gas_owner, gas_cell):
    width = temp_old.shape[1]
    span = min(GROUP, n_surf // 2)
    groups = n_surf // span
    rows = gas_flux.shape[0]
    dma = pltpu.SemaphoreType.DMA

    def box(*shape):
        return pltpu.VMEM((*shape, LANES), F32)

    def fields(index):
        r, c = 24 >> index, 32 >> index
        return [box(r, c), box(r, c), box(r, c), box(r if index == 3 else r + 2, c)]

    def level(index):
        r, c = 24 >> index, 32 >> index
        return [box(r, c)] * 5 + [box(r + 2, c)] * 2

    def ints(*shape):
        return pltpu.VMEM((*shape, LANES), jnp.int32)

    wall = [
        pltpu.VMEM((rows, LANES), jnp.bfloat16), ints(1),
        pltpu.VMEM((groups, rows, LANES), jnp.bfloat16), ints(groups, 1),
        box(span * width + width), box(span, 2 * width),
        dma((2, groups)), dma((2, groups)), dma((span,)), dma((span,)),
    ]
    scratch = [
        box(*temp_old.shape[:2]), box(*temp_old.shape[:2]), ints(width), pltpu.SMEM(zone_props.shape, F32),
        ints(1), ints(1), dma((7,)), wall,
        pltpu.VMEM((3, 9, 32, LANES), jnp.int32), box(26, 32), box(24, 32), box(24, 32),
        *fields(0), *fields(1), *fields(2), *fields(3),
        level(0), level(1), level(2),
        box(24, 32), box(12, 32), box(6, 16), box(3, 8), box(12, 16), box(6, 8), box(3, 4),
        box(2, 2, 1), box(n_depth, 2, 4, 1), box(2, 2, 1), box(2, n_depth, 4, 1),
        box(n_depth, 4, 1), box(n_depth, 4, 1), box(n_depth + 2, 4, 1), box(3, 8),
        box(2, 2, 2, 8), box(2, 2, 2, 8), box(2, 2, 4, 1), box(2, 2, 4, 1),
        dma((8,)), dma((8,)), dma((8,)), dma((8,)),
        dma((3, n_depth, 3)), dma((3, n_depth, 3)), dma((2, 4)), dma((2, 4)),
    ]
    return pl.pallas_call(
        functools.partial(cycles_kernel, n_surf, n_depth, zone_props.shape[1], groups, span),
        out_shape=jax.ShapeDtypeStruct(temp_old.shape, F32),
        in_specs=[pl.BlockSpec(memory_space=pltpu.HBM)] * 7,
        out_specs=pl.BlockSpec(memory_space=pltpu.VMEM),
        scratch_shapes=scratch,
        compiler_params=pltpu.CompilerParams(
            collective_id=0, has_side_effects=True, vmem_limit_bytes=60 * 1024 * 1024),
        name="cycles",
    )(temp_old, virgin, zone, zone_props, gas_flux, gas_owner.reshape(1, rows), gas_cell.reshape(1, rows))


def solution(mesh):
    return jax.shard_map(
        functools.partial(per_device, mesh.shape["surf"], mesh.shape["depth"]),
        mesh=mesh,
        in_specs=(
            P("depth", "surf", None),
            P("depth", "surf", None),
            P("depth", "surf", None),
            P(),
            P("surf", None),
            P("surf", None),
            P("surf"),
        ),
        out_specs=P("depth", "surf", None),
        check_vma=False,
    )
```

```python
import functools

import jax
import jax.numpy as jnp
from jax import lax
from jax.experimental import pallas as pl
from jax.experimental.pallas import tpu as pltpu
from jax.sharding import PartitionSpec as P

MESH = pl.DeviceIdType.MESH
F32 = jnp.float32
OMEGA = 0.8
LANES = 128
GROUP = 16


def roll(value, shift, axis):
    return pltpu.roll(value, shift % value.shape[axis], axis)


class Wall:
    def __init__(self, groups, span, width, refs):
        (self.flux, self.target, self.flux_all, self.target_all, self.partial, self.parts,
         self.send1, self.recv1, self.send2, self.recv2) = refs
        self.groups, self.span, self.width = groups, span, width
        surf, self.depth = lax.axis_index("surf"), lax.axis_index("depth")
        self.group, self.member = surf // span, lax.rem(surf, span)
        self.collects = (self.depth < 2) & (lax.rem(self.group, 2) == self.depth)
        self.owner = self.depth == 0

    def is_self(self, other):
        return self.owner & (lax.rem(self.group, 2) == 0) & (other == self.member)

    def copies1(self, to_group, slot):
        where = (to_group * self.span + self.member, self.depth)
        return [
            pltpu.make_async_remote_copy(
                src_ref=src, dst_ref=dst.at[slot], send_sem=self.send1.at[kind, to_group],
                recv_sem=self.recv1.at[kind, slot], device_id=where, device_id_type=MESH)
            for kind, (src, dst) in enumerate(((self.flux, self.flux_all), (self.target, self.target_all)))
        ]

    def rows_for(self, member):
        return self.partial.at[pl.ds(pl.multiple_of(member * self.width, 8), 2 * self.width)]

    def copy2(self, to_member, slot):
        return pltpu.make_async_remote_copy(
            src_ref=self.rows_for(to_member), dst_ref=self.parts.at[slot],
            send_sem=self.send2.at[to_member], recv_sem=self.recv2.at[slot],
            device_id=(self.group * self.span + to_member, 0), device_id_type=MESH)

    def greet(self, barrier):
        @pl.when(self.collects)
        def _():
            def body(other, carry):
                @pl.when(other != self.group)
                def _():
                    pl.semaphore_signal(
                        barrier, inc=1, device_id=(other * self.span + self.member, self.depth), device_id_type=MESH)
                return carry
            lax.fori_loop(0, self.groups, body, 0)

        @pl.when(self.owner)
        def _():
            def body(other, carry):
                @pl.when(jnp.logical_not(self.is_self(other)))
                def _():
                    pl.semaphore_signal(
                        barrier, inc=1, device_id=(self.group * self.span + other, lax.rem(self.group, 2)),
                        device_id_type=MESH)
                return carry
            lax.fori_loop(0, self.span, body, 0)

    def greetings(self):
        collecting = jnp.where(self.collects, 1, 0)
        from_owners = collecting * (self.span - jnp.where(self.owner, 1, 0))
        return jnp.where(self.depth < 2, self.groups // 2 - collecting, 0) + from_owners

    def each_group(self, act):
        @pl.when(self.depth < 2)
        def _():
            def body(half, carry):
                to_group = 2 * half + self.depth
                @pl.when(to_group != self.group)
                def _():
                    for copy in self.copies1(to_group, self.group):
                        act(copy)
                return carry
            lax.fori_loop(0, self.groups // 2, body, 0)

    def each_member(self, act):
        def body(member, carry):
            @pl.when(jnp.logical_not(self.is_self(member)))
            def _():
                act(self.copy2(member, self.member))
            return carry
        lax.fori_loop(0, self.span, body, 0)

    def collect(self):
        @pl.when(self.collects)
        def _():
            self.flux_all[self.group] = self.flux[...]
            self.target_all[self.group] = self.target[...]
            self.partial[...] = jnp.zeros_like(self.partial)
            rows = self.partial.shape[0]
            first = self.group * (self.span * self.width) - self.width // 2
            ids = first + lax.broadcasted_iota(jnp.int32, (rows, LANES), 0)

            def add(other, carry):
                @pl.when(other != self.group)
                def _():
                    for copy in self.copies1(other, other):
                        copy.wait_recv()
                placing = jnp.where(ids == self.target_all[other], 1.0, 0.0).astype(jnp.bfloat16)
                self.partial[...] += jnp.dot(placing, self.flux_all[other], preferred_element_type=F32)
                return carry
            lax.fori_loop(0, self.groups, add, 0)

            @pl.when(self.is_self(self.member))
            def _():
                self.parts[self.member] = self.rows_for(self.member)[...]
            self.each_member(lambda copy: copy.start())

    def add_to(self, source, row):
        @pl.when(self.owner)
        def _():
            def body(other, carry):
                @pl.when(jnp.logical_not(self.is_self(other)))
                def _():
                    self.copy2(other, other).wait_recv()
                source[row] = source[row] + self.parts[other]
                return carry
            lax.fori_loop(0, self.span, body, 0)

    def finish(self):
        self.each_group(lambda copy: copy.wait_send())

        @pl.when(self.collects)
        def _():
            self.each_member(lambda copy: copy.wait_send())


SIDES = [(-1, 0), (1, 0), (-1, -1), (-1, 1), (1, -1), (1, 1), (0, -1), (0, 1)]


class Level:
    def __init__(self, refs, halo_z, halo_x):
        self.C, self.WX, self.WY, self.WI, self.B, self.WZ, self.U = refs
        self.rows, self.cols = self.C.shape[0], self.C.shape[1]
        self.halo_z, self.halo_x = halo_z, halo_x


def residual(level, field, first, count):
    here, up, down = (pl.ds(first + shift, count) for shift in (1, 2, 0))
    own = pl.ds(first, count)
    mid = field[here]
    wx, wy = level.WX[own], level.WY[own]
    total = level.B[own] - level.C[own] * mid
    total = total + level.WZ[here] * field[up] + level.WZ[down] * field[down]
    total = total + wx * roll(mid, -1, 1) + roll(wx * mid, 1, 1)
    return total + wy * roll(mid, -1, 2) + roll(wy * mid, 1, 2)


def restrict_into(source, skip, scratch, target, target_skip):
    rows, cols = scratch.shape[0], scratch.shape[1]
    for row in range(rows):
        scratch[row] = source[skip + 2 * row] + source[skip + 2 * row + 1]
    even = scratch[:, pl.ds(0, cols // 2, stride=2), :]
    odd = scratch[:, pl.ds(1, cols // 2, stride=2), :]
    target[pl.ds(target_skip, rows)] = 0.25 * (even + odd)


def prolong_onto(level, coarse, scratch, first, count):
    cols = scratch.shape[1]
    low, number = first // 2, count // 2
    part = coarse[pl.ds(low, number)]
    scratch[pl.ds(low, number), pl.ds(0, cols // 2, stride=2), :] = part
    scratch[pl.ds(low, number), pl.ds(1, cols // 2, stride=2), :] = part
    for row in range(low, low + number):
        wide = scratch[row]
        level.U[1 + 2 * row] = level.U[1 + 2 * row] + wide
        level.U[2 + 2 * row] = level.U[2 + 2 * row] + wide


def cycles_kernel(n_surf, n_depth, n_zones, groups, span,
                  temp_hbm, virgin_hbm, zone_hbm, props_hbm, flux_hbm, owner_hbm, cell_hbm, out_ref,
                  temp_ref, virgin_ref, zone_ref, props_ref, owner_ref, cell_ref, in_sem, wall_refs,
                  packed, guess, temp, virgin,
                  fd0, fx0, fy0, fz0, fd1, fx1, fy1, fz1, fd2, fx2, fy2, fz2, fd3, fx3, fy3, fz3,
                  l0, l1, l2, res, t0, t1, t2, v1, v2, b3,
                  coef_own, coef_all, rhs_own, rhs_all, ratio, inverse, solved, e2,
                  z_out, z_in, x_out, x_in,
                  s_send, s_recv, e_send, e_recv, g_send, g_recv, h_send, h_recv):
    surf, depth = lax.axis_index("surf"), lax.axis_index("depth")

    def at(dz, dx):
        return (lax.rem(surf + dx + n_surf, n_surf), lax.rem(depth + dz + n_depth, n_depth))

    levels = [Level(refs, 8 >> index, 8 >> index) for index, refs in enumerate((l0, l1, l2))]
    top, mid, low = levels

    width = out_ref.shape[1]
    wall = Wall(groups, span, width, wall_refs)
    inputs = [
        pltpu.make_async_copy(src, dst, in_sem.at[index])
        for index, (src, dst) in enumerate((
            (temp_hbm, temp_ref), (virgin_hbm, virgin_ref), (zone_hbm.at[0], zone_ref), (flux_hbm, wall.flux),
            (owner_hbm, owner_ref), (cell_hbm, cell_ref), (props_hbm, props_ref)))
    ]
    for copy in inputs:
        copy.start()
    for columns in (pl.ds(0, 8), pl.ds(24, 8)):
        for block in (0, 2):
            packed[block, :, columns] = jnp.zeros((10, 8, LANES), jnp.int32)
            guess[pl.ds(1 + 8 * block, 8), columns] = jnp.zeros((8, 8, LANES), F32)

    barrier = pltpu.get_barrier_semaphore()

    def greet(step, carry):
        dz = n_depth // 2 + jnp.where(lax.rem(step, 2) == 1, (step + 1) // 2, -(step // 2))
        for dx in (-1, 0, 1):
            pl.semaphore_signal(barrier, inc=1, device_id=at(dz, dx), device_id_type=MESH)
        return carry

    lax.fori_loop(0, n_depth - 1, greet, 0)
    for dx in (-1, 1):
        pl.semaphore_signal(barrier, inc=1, device_id=at(0, dx), device_id_type=MESH)
    wall.greet(barrier)
    for copy in inputs:
        copy.wait()
    wall.target[...] = owner_ref[...] * width + cell_ref[...]

    own_t = temp_ref[...]
    own_v = virgin_ref[...]
    code_t = ((own_t - 0.5) * (65535.0 / 1.5) + 0.5).astype(jnp.int32)
    code_v = ((own_v - 0.2) * (65535.0 / 0.8) + 0.5).astype(jnp.int32)
    packed[1, 1:9, 8:24] = jnp.left_shift(code_t, 16) | code_v
    packed[1, 0, 8:24] = zone_ref[...]
    packed[1, 9, 8:24] = zone_ref[...]
    pl.semaphore_wait(barrier, 3 * n_depth - 1 + wall.greetings())

    src_x = {-1: (8, 8), 0: (8, 16), 1: (16, 8)}
    dst_x = {-1: 24, 0: 8, 1: 0}

    def ring_copy(index, ref_src, ref_dst, send, recv, dz, dx):
        return pltpu.make_async_remote_copy(
            src_ref=ref_src, dst_ref=ref_dst, send_sem=send.at[index], recv_sem=recv.at[index],
            device_id=at(dz, dx), device_id_type=MESH)

    def pieces(sizes, dz, dx):
        found = []
        for first_row, last_row, columns in sizes:
            first = first_row if dz < 0 else 9 - last_row
            count = last_row - first_row + 1
            low, _ = src_x[dx]
            skip = 0 if dx < 0 else 8 - columns
            found.append((first, count, low + skip, dst_x[dx] + skip, columns))
        return found

    def setup_copies():
        copies = []
        for dz, dx in SIDES:
            if dz and dx:
                near, far = pieces(((1, 4, 8), (5, 8, 4)), dz, dx)
                near = (near[0] - (1 if dz < 0 else 0), near[1] + 1) + near[2:]
                parts = [near, far]
            else:
                parts = [(1 if dz > 0 else 0, 9, src_x[dx][0], dst_x[dx], src_x[dx][1])]
            for row, rows, src, dst, columns in parts:
                copies.append(((dz, dx), ring_copy(
                    len(copies), packed.at[1, pl.ds(row, rows), pl.ds(src, columns)],
                    packed.at[1 - dz, pl.ds(row, rows), pl.ds(dst, columns)], s_send, s_recv, dz, dx)))
        return copies

    def guess_copies():
        copies = []
        for dz, dx in SIDES:
            if dz and dx:
                parts = pieces(((1, 3, 7), (4, 7, 4)), dz, dx)
            else:
                parts = [(1, 8, src_x[dx][0], dst_x[dx], src_x[dx][1])]
            for row, rows, src, dst, columns in parts:
                copies.append(ring_copy(
                    len(copies), guess.at[pl.ds(8 + row, rows), pl.ds(src, columns)],
                    guess.at[pl.ds(8 * (1 - dz) + row, rows), pl.ds(dst, columns)], e_send, e_recv, dz, dx))
        return copies

    ring_inputs, ring_guess = setup_copies(), guess_copies()
    wall.each_group(lambda copy: copy.start())
    for _, copy in ring_inputs:
        copy.start()

    def column_mask(level):
        column = lax.broadcasted_iota(jnp.int32, (level.cols, LANES), 0)
        first, last = level.halo_x, level.cols - level.halo_x
        inside = ((column >= first) | (surf > 0)) & ((column < last) | (surf < n_surf - 1))
        return jnp.where(inside, 1.0, 0.0)

    row_mask = [jnp.where(depth > 0, 1.0, 0.0), jnp.float32(1.0), jnp.where(depth < n_depth - 1, 1.0, 0.0)]
    masks = [column_mask(level) for level in levels]
    for level in levels:
        zero = jnp.zeros((level.cols, LANES), F32)
        level.WZ[0] = zero
        level.U[0] = zero
        level.U[level.rows + 1] = zero
    for ref in (fz0, fz1, fz2):
        ref[0] = jnp.zeros(ref.shape[1:], F32)
        ref[ref.shape[0] - 1] = jnp.zeros(ref.shape[1:], F32)
    guess[0] = jnp.zeros(guess.shape[1:], F32)
    guess[25] = jnp.zeros(guess.shape[1:], F32)
    solved[0] = jnp.zeros(solved.shape[1:], F32)
    solved[n_depth + 1] = jnp.zeros(solved.shape[1:], F32)

    wall.collect()

    for block in (1, 0, 2):
        for (dz, _), copy in ring_inputs:
            if dz == 1 - block:
                copy.wait_recv()
        code = packed[block, 1:9]
        rows = pl.ds(8 * block, 8)
        temp[rows] = 0.5 + lax.shift_right_logical(code, 16).astype(F32) * (1.5 / 65535.0)
        virgin[rows] = 0.2 + (code & 0xFFFF).astype(F32) * (0.8 / 65535.0)
        if block == 1:
            temp[rows, 8:24] = own_t
            virgin[rows, 8:24] = own_v
        zone = packed[block, 9 if block == 0 else 0]
        inside = masks[0] * row_mask[block]
        props = [jnp.zeros((top.cols, LANES), F32) for _ in range(4)]
        for number in range(n_zones):
            hit = zone == number
            props = [jnp.where(hit, props_ref[kind, number], props[kind]) for kind in range(4)]
        props = [value * inside for value in props]
        for row in range(8 * block, 8 * block + 8, 2):
            rows = pl.ds(row, 2)
            t, v = temp[rows], virgin[rows]
            squared = t * t
            blend = (0.5 + squared) * (0.4 + 0.6 * v)
            rate = 8.0 * v * jnp.exp(-3.0 / t)
            fz0[pl.ds(row + 1, 2)] = props[0] * blend
            fx0[rows] = props[1] * blend
            fy0[rows] = props[2] * blend
            fd0[rows] = (props[3] * (0.5 + v) + 6.0 * rate / squared) * inside
            top.B[rows] = -2.0 * rate * inside

    fields = [(fd0, fx0, fy0, fz0), (fd1, fx1, fy1, fz1), (fd2, fx2, fy2, fz2), (fd3, fx3, fy3, fz3)]
    scratches = (t0, t1, t2)

    for index, level in enumerate(levels):
        fd, fx, fy, fz = fields[index]
        half = 0.5 * 0.25**index
        step = min(4, level.halo_z)
        lane = lax.broadcasted_iota(jnp.int32, (step, level.cols, LANES), 2)
        for row in range(0, level.rows, step):
            rows = pl.ds(row, step)
            inside = masks[index] * row_mask[row // level.halo_z]
            here = fz[pl.ds(row + 1, step)]
            lower = half * (here + fz[rows])
            upper = half * (here + fz[pl.ds(row + 2, step)])
            level.WZ[pl.ds(row + 1, step)] = upper
            across = fx[rows]
            east = half * (across + roll(across, -1, 1))
            west = roll(east, 1, 1)
            level.WX[rows] = east
            along = fy[rows]
            north = 0.5 * (along + jnp.where(lane == LANES - 1, 0.0, roll(along, -1, 2)))
            south = 0.5 * (along + jnp.where(lane == 0, 0.0, roll(along, 1, 2)))
            level.WY[rows] = jnp.where(lane == LANES - 1, 0.0, north)
            centre = fd[rows] + lower + upper + west + east + south + north
            level.C[rows] = centre
            level.WI[rows] = jnp.where((inside > 0.0)[None], OMEGA / centre, 0.0)
        for kind in range(4):
            skip = 1 if kind == 3 else 0
            target_skip = 1 if kind == 3 and index < 2 else 0
            restrict_into(fields[index][kind], skip, scratches[index], fields[index + 1][kind], target_skip)

    half = 0.5 * 0.25**3
    centre_z, centre_x, centre_y = fz3[1, 1:3], fx3[1, 1:3], fy3[1, 1:3]
    lane = lax.broadcasted_iota(jnp.int32, (2, LANES), 1)
    lower = half * (centre_z + fz3[0, 1:3])
    upper = half * (centre_z + fz3[2, 1:3])
    west = half * (centre_x + fx3[1, 0:2])
    east = half * (centre_x + fx3[1, 2:4])
    north = 0.5 * (centre_y + jnp.where(lane == LANES - 1, 0.0, roll(centre_y, -1, 1)))
    south = 0.5 * (centre_y + jnp.where(lane == 0, 0.0, roll(centre_y, 1, 1)))
    centre = fd3[1, 1:3] + lower + upper + west + east + south + north
    for column in range(2):
        coef_own[0, column] = centre[column : column + 1]
        coef_own[1, column] = upper[column : column + 1]

    source_column = {-1: (0, 1), 0: (0, 2), 1: (1, 1)}
    landing_column = {-1: 3, 0: 1, 1: 0}

    def column_copy(phase, dz, dx):
        first, count = source_column[dx]
        if phase == 0:
            src, dst = coef_own.at[:, pl.ds(first, count)], coef_all.at[depth, :, pl.ds(landing_column[dx], count)]
        else:
            src = rhs_own.at[phase - 1, pl.ds(first, count)]
            dst = rhs_all.at[phase - 1, depth, pl.ds(landing_column[dx], count)]
        return pltpu.make_async_remote_copy(
            src_ref=src, dst_ref=dst, send_sem=g_send.at[phase, dz, dx + 1],
            recv_sem=g_recv.at[phase, dz, dx + 1], device_id=at(dz, dx), device_id_type=MESH)

    def each_column(phase, act):
        for dx in (-1, 1):
            act(column_copy(phase, 0, dx))

        def body(dz, carry):
            for dx in (-1, 0, 1):
                act(column_copy(phase, dz, dx))
            return carry

        lax.fori_loop(1, n_depth, body, 0)

    each_column(0, lambda copy: copy.start())
    coef_all[depth, :, 1:3] = coef_own[...]

    wall.add_to(top.B, 8)

    def down(level, scratch, coarse_rhs, chunk):
        for row in range(0, level.rows, chunk):
            res[pl.ds(row, chunk), 0 : level.cols] = residual(level, level.U, row, chunk)
        restrict_into(res.at[:, pl.ds(0, level.cols)], 0, scratch, coarse_rhs, 0)

    def near_copies(cycle):
        pairs = []
        for index, (dz, dx) in enumerate(((-1, 0), (1, 0), (0, -1), (0, 1))):
            side = index % 2
            out, into = (z_out, z_in) if dz else (x_out, x_in)
            pairs.append(pltpu.make_async_remote_copy(
                src_ref=out.at[cycle, side], dst_ref=into.at[cycle, 1 - side],
                send_sem=h_send.at[cycle, index], recv_sem=h_recv.at[cycle, index],
                device_id=at(dz, dx), device_id_type=MESH))
        return pairs

    def run_cycle(cycle, last):
        down(top, t0, mid.B, 4)
        mid.U[1:13] = mid.WI[...] * mid.B[...]
        down(mid, t1, low.B, 4)
        low.U[1:7] = low.WI[...] * low.B[...]
        down(low, t2, b3, 6)
        for column in range(2):
            rhs_own[cycle, column] = b3[1, 1 + column : 2 + column]
        each_column(1 + cycle, lambda copy: copy.start())
        z_out[cycle, 0, 0] = low.B[2]
        z_out[cycle, 0, 1] = low.U[4]
        z_out[cycle, 1, 0] = low.B[3]
        z_out[cycle, 1, 1] = low.U[3]
        for row in range(4):
            x_out[cycle, 0, row] = low.U[2 + row, 3:4]
            x_out[cycle, 1, row] = low.U[2 + row, 4:5]
        near = near_copies(cycle)
        for copy in near:
            copy.start()
        rhs_all[cycle, depth, 1:3] = rhs_own[cycle]

        if cycle == 0:
            each_column(0, lambda copy: copy.wait_recv())
            inv = 1.0 / coef_all[0, 0]
            inverse[0] = inv
            ratio[0] = coef_all[0, 1] * inv
            for row in range(1, n_depth):
                inv = 1.0 / (coef_all[row, 0] - coef_all[row - 1, 1] * ratio[row - 1])
                inverse[row] = inv
                ratio[row] = coef_all[row, 1] * inv

        for copy in near:
            copy.wait_recv()
        low.B[1] = z_in[cycle, 0, 0]
        low.B[4] = z_in[cycle, 1, 0]
        low.U[2] = low.WI[1] * low.B[1]
        low.U[5] = low.WI[4] * low.B[4]
        low.U[1] = z_in[cycle, 0, 1] * (masks[2] * row_mask[0])
        low.U[6] = z_in[cycle, 1, 1] * (masks[2] * row_mask[2])
        for row in range(4):
            block = (0, 1, 1, 2)[row]
            first = jnp.where(surf > 0, 1.0, 0.0) * row_mask[block]
            final = jnp.where(surf < n_surf - 1, 1.0, 0.0) * row_mask[block]
            low.U[2 + row, 0:1] = x_in[cycle, 0, row] * first
            low.U[2 + row, 7:8] = x_in[cycle, 1, row] * final

        each_column(1 + cycle, lambda copy: copy.wait_recv())
        value = rhs_all[cycle, 0] * inverse[0]
        values = [value]
        for row in range(1, n_depth):
            value = (rhs_all[cycle, row] + coef_all[row - 1, 1] * value) * inverse[row]
            values.append(value)
        later = values[-1]
        solved[n_depth] = later
        for row in range(n_depth - 2, -1, -1):
            later = values[row] + ratio[row] * later
            solved[row + 1] = later
        for row in range(3):
            for column in range(4):
                value = solved[depth + row, column]
                if column == 0:
                    value = value * jnp.where(surf > 0, 1.0, 0.0)
                if column == 3:
                    value = value * jnp.where(surf < n_surf - 1, 1.0, 0.0)
                e2[row, 2 * column : 2 * column + 2] = jnp.broadcast_to(value, (2, LANES))
        for row in range(3):
            wide = e2[row]
            low.U[1 + 2 * row] = low.U[1 + 2 * row] + wide
            low.U[2 + 2 * row] = low.U[2 + 2 * row] + wide
        v2[...] = low.U[1:7] + low.WI[...] * residual(low, low.U, 0, 6)
        prolong_onto(mid, v2, t1, 2, 8)
        v1[2:10] = mid.U[3:11] + mid.WI[2:10] * residual(mid, mid.U, 2, 8)
        prolong_onto(top, v1, t0, 6, 12)
        for row in range(8, 16, 4):
            rows = pl.ds(row, 4)
            new = top.U[pl.ds(row + 1, 4)] + top.WI[rows] * residual(top, top.U, row, 4)
            if last:
                out_ref[pl.ds(row - 8, 4)] = new[:, 8:24]
            else:
                guess[pl.ds(row + 1, 4), 8:24] = new[:, 8:24]

    top.U[1:25] = top.WI[...] * top.B[...]
    run_cycle(0, False)
    for copy in ring_guess:
        copy.start()
    for copy in ring_guess:
        copy.wait_recv()
    for block in range(3):
        rows = pl.ds(1 + 8 * block, 8)
        if block == 1:
            for columns, inside in ((slice(0, 8), surf > 0), (slice(24, 32), surf < n_surf - 1)):
                guess[rows, columns] = guess[rows, columns] * jnp.where(inside, 1.0, 0.0)
        else:
            guess[rows] = guess[rows] * (masks[0] * row_mask[block])
    for row in range(0, 24, 4):
        rows, padded = pl.ds(row, 4), pl.ds(row + 1, 4)
        top.U[padded] = guess[padded] + top.WI[rows] * residual(top, guess, row, 4)
    run_cycle(1, True)

    for copy in [copy for _, copy in ring_inputs] + ring_guess:
        copy.wait_send()
    wall.finish()
    for phase in range(3):
        each_column(phase, lambda copy: copy.wait_send())
    for cycle in range(2):
        for copy in near_copies(cycle):
            copy.wait_send()


def per_device(n_surf, n_depth, temp_old, virgin, zone, zone_props, gas_flux, gas_owner, gas_cell):
    width = temp_old.shape[1]
    span = min(GROUP, n_surf // 2)
    groups = n_surf // span
    rows = gas_flux.shape[0]
    dma = pltpu.SemaphoreType.DMA

    def box(*shape):
        return pltpu.VMEM((*shape, LANES), F32)

    def fields(index):
        r, c = 24 >> index, 32 >> index
        return [box(r, c), box(r, c), box(r, c), box(r if index == 3 else r + 2, c)]

    def level(index):
        r, c = 24 >> index, 32 >> index
        return [box(r, c)] * 5 + [box(r + 2, c)] * 2

    def ints(*shape):
        return pltpu.VMEM((*shape, LANES), jnp.int32)

    wall = [
        pltpu.VMEM((rows, LANES), jnp.bfloat16), ints(1),
        pltpu.VMEM((groups, rows, LANES), jnp.bfloat16), ints(groups, 1),
        box(span * width + width), box(span, 2 * width),
        dma((2, groups)), dma((2, groups)), dma((span,)), dma((span,)),
    ]
    scratch = [
        box(*temp_old.shape[:2]), box(*temp_old.shape[:2]), ints(width), pltpu.SMEM(zone_props.shape, F32),
        ints(1), ints(1), dma((7,)), wall,
        pltpu.VMEM((3, 10, 32, LANES), jnp.int32), box(26, 32), box(24, 32), box(24, 32),
        *fields(0), *fields(1), *fields(2), *fields(3),
        level(0), level(1), level(2),
        box(24, 32), box(12, 32), box(6, 16), box(3, 8), box(12, 16), box(6, 8), box(3, 4),
        box(2, 2, 1), box(n_depth, 2, 4, 1), box(2, 2, 1), box(2, n_depth, 4, 1),
        box(n_depth, 4, 1), box(n_depth, 4, 1), box(n_depth + 2, 4, 1), box(3, 8),
        box(2, 2, 2, 8), box(2, 2, 2, 8), box(2, 2, 4, 1), box(2, 2, 4, 1),
        dma((12,)), dma((12,)), dma((12,)), dma((12,)),
        dma((3, n_depth, 3)), dma((3, n_depth, 3)), dma((2, 4)), dma((2, 4)),
    ]
    return pl.pallas_call(
        functools.partial(cycles_kernel, n_surf, n_depth, zone_props.shape[1], groups, span),
        out_shape=jax.ShapeDtypeStruct(temp_old.shape, F32),
        in_specs=[pl.BlockSpec(memory_space=pltpu.HBM)] * 7,
        out_specs=pl.BlockSpec(memory_space=pltpu.VMEM),
        scratch_shapes=scratch,
        compiler_params=pltpu.CompilerParams(
            collective_id=0, has_side_effects=True, vmem_limit_bytes=48 * 1024 * 1024),
        name="cycles",
    )(*[pltpu.with_memory_space_constraint(a, pltpu.HBM) for a in (temp_old, virgin, zone, zone_props, gas_flux, gas_owner.reshape(1, rows), gas_cell.reshape(1, rows))])


def solution(mesh):
    return jax.shard_map(
        functools.partial(per_device, mesh.shape["surf"], mesh.shape["depth"]),
        mesh=mesh,
        in_specs=(
            P("depth", "surf", None),
            P("depth", "surf", None),
            P("depth", "surf", None),
            P(),
            P("surf", None),
            P("surf", None),
            P("surf"),
        ),
        out_specs=P("depth", "surf", None),
        check_vma=False,
    )
```

```python
import functools

import jax
import jax.numpy as jnp
from jax import lax
from jax.experimental import pallas as pl
from jax.experimental.pallas import tpu as pltpu
from jax.sharding import PartitionSpec as P

MESH = pl.DeviceIdType.MESH
F32 = jnp.float32
OMEGA = 0.8
LANES = 128
GROUP = 16


def roll(value, shift, axis):
    return pltpu.roll(value, shift % value.shape[axis], axis)


class Wall:
    def __init__(self, groups, span, width, refs):
        (self.flux, self.target, self.flux_all, self.target_all, self.partial, self.parts,
         self.send1, self.recv1, self.send2, self.recv2) = refs
        self.groups, self.span, self.width = groups, span, width
        surf, self.depth = lax.axis_index("surf"), lax.axis_index("depth")
        self.group, self.member = surf // span, lax.rem(surf, span)
        self.collects = (self.depth < 2) & (lax.rem(self.group, 2) == self.depth)
        self.owner = self.depth == 0

    def is_self(self, other):
        return self.owner & (lax.rem(self.group, 2) == 0) & (other == self.member)

    def copies1(self, to_group, slot):
        where = (to_group * self.span + self.member, self.depth)
        return [
            pltpu.make_async_remote_copy(
                src_ref=src, dst_ref=dst.at[slot], send_sem=self.send1.at[kind, to_group],
                recv_sem=self.recv1.at[kind, slot], device_id=where, device_id_type=MESH)
            for kind, (src, dst) in enumerate(((self.flux, self.flux_all), (self.target, self.target_all)))
        ]

    def rows_for(self, member):
        return self.partial.at[pl.ds(pl.multiple_of(member * self.width, 8), 2 * self.width)]

    def copy2(self, to_member, slot):
        return pltpu.make_async_remote_copy(
            src_ref=self.rows_for(to_member), dst_ref=self.parts.at[slot],
            send_sem=self.send2.at[to_member], recv_sem=self.recv2.at[slot],
            device_id=(self.group * self.span + to_member, 0), device_id_type=MESH)

    def greet(self, barrier):
        @pl.when(self.collects)
        def _():
            def body(other, carry):
                @pl.when(other != self.group)
                def _():
                    pl.semaphore_signal(
                        barrier, inc=1, device_id=(other * self.span + self.member, self.depth), device_id_type=MESH)
                return carry
            lax.fori_loop(0, self.groups, body, 0)

        @pl.when(self.owner)
        def _():
            def body(other, carry):
                @pl.when(jnp.logical_not(self.is_self(other)))
                def _():
                    pl.semaphore_signal(
                        barrier, inc=1, device_id=(self.group * self.span + other, lax.rem(self.group, 2)),
                        device_id_type=MESH)
                return carry
            lax.fori_loop(0, self.span, body, 0)

    def greetings(self):
        collecting = jnp.where(self.collects, 1, 0)
        from_owners = collecting * (self.span - jnp.where(self.owner, 1, 0))
        return jnp.where(self.depth < 2, self.groups // 2 - collecting, 0) + from_owners

    def each_group(self, act):
        @pl.when(self.depth < 2)
        def _():
            def body(half, carry):
                to_group = 2 * half + self.depth
                @pl.when(to_group != self.group)
                def _():
                    for copy in self.copies1(to_group, self.group):
                        act(copy)
                return carry
            lax.fori_loop(0, self.groups // 2, body, 0)

    def each_member(self, act):
        def body(member, carry):
            @pl.when(jnp.logical_not(self.is_self(member)))
            def _():
                act(self.copy2(member, self.member))
            return carry
        lax.fori_loop(0, self.span, body, 0)

    def collect(self):
        @pl.when(self.collects)
        def _():
            self.flux_all[self.group] = self.flux[...]
            self.target_all[self.group] = self.target[...]
            self.partial[...] = jnp.zeros_like(self.partial)
            rows = self.partial.shape[0]
            first = self.group * (self.span * self.width) - self.width // 2
            ids = first + lax.broadcasted_iota(jnp.int32, (rows, LANES), 0)

            def add(other, carry):
                @pl.when(other != self.group)
                def _():
                    for copy in self.copies1(other, other):
                        copy.wait_recv()
                placing = jnp.where(ids == self.target_all[other], 1.0, 0.0).astype(jnp.bfloat16)
                self.partial[...] += jnp.dot(placing, self.flux_all[other], preferred_element_type=F32)
                return carry
            lax.fori_loop(0, self.groups, add, 0)

            @pl.when(self.is_self(self.member))
            def _():
                self.parts[self.member] = self.rows_for(self.member)[...]
            self.each_member(lambda copy: copy.start())

    def add_to(self, source, row):
        @pl.when(self.owner)
        def _():
            def body(other, carry):
                @pl.when(jnp.logical_not(self.is_self(other)))
                def _():
                    self.copy2(other, other).wait_recv()
                source[row] = source[row] + self.parts[other]
                return carry
            lax.fori_loop(0, self.span, body, 0)

    def finish(self):
        self.each_group(lambda copy: copy.wait_send())

        @pl.when(self.collects)
        def _():
            self.each_member(lambda copy: copy.wait_send())


SIDES = [(-1, 0), (1, 0), (-1, -1), (-1, 1), (1, -1), (1, 1), (0, -1), (0, 1)]


class Level:
    def __init__(self, refs, halo_z, halo_x):
        self.C, self.WX, self.WY, self.WI, self.B, self.WZ, self.U = refs
        self.rows, self.cols = self.C.shape[0], self.C.shape[1]
        self.halo_z, self.halo_x = halo_z, halo_x


def residual(level, field, first, count):
    here, up, down = (pl.ds(first + shift, count) for shift in (1, 2, 0))
    own = pl.ds(first, count)
    mid = field[here]
    wx, wy = level.WX[own], level.WY[own]
    total = level.B[own] - level.C[own] * mid
    total = total + level.WZ[here] * field[up] + level.WZ[down] * field[down]
    total = total + wx * roll(mid, -1, 1) + roll(wx * mid, 1, 1)
    return total + wy * roll(mid, -1, 2) + roll(wy * mid, 1, 2)


def restrict_into(source, skip, scratch, target, target_skip):
    rows, cols = scratch.shape[0], scratch.shape[1]
    for row in range(rows):
        scratch[row] = source[skip + 2 * row] + source[skip + 2 * row + 1]
    even = scratch[:, pl.ds(0, cols // 2, stride=2), :]
    odd = scratch[:, pl.ds(1, cols // 2, stride=2), :]
    target[pl.ds(target_skip, rows)] = 0.25 * (even + odd)


def prolong_onto(level, coarse, scratch, first, count):
    cols = scratch.shape[1]
    low, number = first // 2, count // 2
    part = coarse[pl.ds(low, number)]
    scratch[pl.ds(low, number), pl.ds(0, cols // 2, stride=2), :] = part
    scratch[pl.ds(low, number), pl.ds(1, cols // 2, stride=2), :] = part
    for row in range(low, low + number):
        wide = scratch[row]
        level.U[1 + 2 * row] = level.U[1 + 2 * row] + wide
        level.U[2 + 2 * row] = level.U[2 + 2 * row] + wide


def cycles_kernel(n_surf, n_depth, n_zones, groups, span,
                  temp_hbm, virgin_hbm, zone_hbm, props_hbm, flux_hbm, owner_hbm, cell_hbm, out_ref,
                  temp_ref, virgin_ref, zone_ref, props_ref, owner_ref, cell_ref, in_sem, wall_refs,
                  packed, zones, guess, temp, virgin,
                  fd0, fx0, fy0, fz0, fd1, fx1, fy1, fz1, fd2, fx2, fy2, fz2, fd3, fx3, fy3, fz3,
                  l0, l1, l2, res, t0, t1, t2, v1, v2, b3,
                  coef_own, coef_all, rhs_own, rhs_all, ratio, inverse, solved, e2,
                  z_out, z_in, x_out, x_in,
                  s_send, s_recv, e_send, e_recv, g_send, g_recv, h_send, h_recv):
    surf, depth = lax.axis_index("surf"), lax.axis_index("depth")

    def at(dz, dx):
        return (lax.rem(surf + dx + n_surf, n_surf), lax.rem(depth + dz + n_depth, n_depth))

    levels = [Level(refs, 8 >> index, 8 >> index) for index, refs in enumerate((l0, l1, l2))]
    top, mid, low = levels

    width = out_ref.shape[1]
    wall = Wall(groups, span, width, wall_refs)
    inputs = [
        pltpu.make_async_copy(src, dst, in_sem.at[index])
        for index, (src, dst) in enumerate((
            (temp_hbm, temp_ref), (virgin_hbm, virgin_ref), (zone_hbm.at[0], zone_ref), (flux_hbm, wall.flux),
            (owner_hbm, owner_ref), (cell_hbm, cell_ref), (props_hbm, props_ref)))
    ]
    for copy in inputs:
        copy.start()
    for columns in (pl.ds(0, 8), pl.ds(24, 8)):
        for block in (0, 2):
            packed[block, :, columns] = jnp.zeros((8, 8, LANES), jnp.int32)
            guess[pl.ds(1 + 8 * block, 8), columns] = jnp.zeros((8, 8, LANES), F32)

    barrier = pltpu.get_barrier_semaphore()

    def greet(step, carry):
        dz = n_depth // 2 + jnp.where(lax.rem(step, 2) == 1, (step + 1) // 2, -(step // 2))
        for dx in (-1, 0, 1):
            pl.semaphore_signal(barrier, inc=1, device_id=at(dz, dx), device_id_type=MESH)
        return carry

    lax.fori_loop(0, n_depth - 1, greet, 0)
    for dx in (-1, 1):
        pl.semaphore_signal(barrier, inc=1, device_id=at(0, dx), device_id_type=MESH)
    wall.greet(barrier)
    for copy in inputs:
        copy.wait()
    wall.target[...] = owner_ref[...] * width + cell_ref[...]

    own_t = temp_ref[...]
    own_v = virgin_ref[...]
    code_t = ((own_t - 0.5) * (65535.0 / 1.5) + 0.5).astype(jnp.int32)
    code_v = ((own_v - 0.2) * (65535.0 / 0.8) + 0.5).astype(jnp.int32)
    packed[1, :, 8:24] = jnp.left_shift(code_t, 16) | code_v
    for half in range(2):
        zones[1, 1 + half] = zone_ref[8 * half : 8 * half + 1]
    pl.semaphore_wait(barrier, 3 * n_depth - 1 + wall.greetings())

    src_x = {-1: (8, 8), 0: (8, 16), 1: (16, 8)}
    dst_x = {-1: 24, 0: 8, 1: 0}

    def ring_copy(index, ref_src, ref_dst, send, recv, dz, dx):
        return pltpu.make_async_remote_copy(
            src_ref=ref_src, dst_ref=ref_dst, send_sem=send.at[index], recv_sem=recv.at[index],
            device_id=at(dz, dx), device_id_type=MESH)

    def pieces(sizes, dz, dx):
        found = []
        for first_row, last_row, columns in sizes:
            first = first_row if dz < 0 else 9 - last_row
            count = last_row - first_row + 1
            low, _ = src_x[dx]
            skip = 0 if dx < 0 else 8 - columns
            found.append((first, count, low + skip, dst_x[dx] + skip, columns))
        return found

    def setup_copies():
        copies = []
        for dz, dx in SIDES:
            if dz and dx:
                parts = pieces(((1, 4, 8), (5, 8, 4)), dz, dx)
            else:
                parts = [(1, 8, src_x[dx][0], dst_x[dx], src_x[dx][1])]
            for row, rows, src, dst, columns in parts:
                copies.append(((dz, dx), ring_copy(
                    len(copies), packed.at[1, pl.ds(row - 1, rows), pl.ds(src, columns)],
                    packed.at[1 - dz, pl.ds(row - 1, rows), pl.ds(dst, columns)], s_send, s_recv, dz, dx)))
            src, count, dst = {-1: (1, 1, 3), 0: (1, 2, 1), 1: (2, 1, 0)}[dx]
            copies.append(((dz, dx), ring_copy(
                len(copies), zones.at[1, pl.ds(src, count)], zones.at[1 - dz, pl.ds(dst, count)],
                s_send, s_recv, dz, dx)))
        return copies

    def guess_copies():
        copies = []
        for dz, dx in SIDES:
            if dz and dx:
                parts = pieces(((1, 2, 7), (3, 4, 5), (5, 7, 3)), dz, dx)
            else:
                parts = [(1, 8, src_x[dx][0], dst_x[dx], src_x[dx][1])]
            for row, rows, src, dst, columns in parts:
                copies.append(ring_copy(
                    len(copies), guess.at[pl.ds(8 + row, rows), pl.ds(src, columns)],
                    guess.at[pl.ds(8 * (1 - dz) + row, rows), pl.ds(dst, columns)], e_send, e_recv, dz, dx))
        return copies

    ring_inputs, ring_guess = setup_copies(), guess_copies()
    wall.each_group(lambda copy: copy.start())
    for _, copy in ring_inputs:
        copy.start()

    def column_mask(level):
        column = lax.broadcasted_iota(jnp.int32, (level.cols, LANES), 0)
        first, last = level.halo_x, level.cols - level.halo_x
        inside = ((column >= first) | (surf > 0)) & ((column < last) | (surf < n_surf - 1))
        return jnp.where(inside, 1.0, 0.0)

    row_mask = [jnp.where(depth > 0, 1.0, 0.0), jnp.float32(1.0), jnp.where(depth < n_depth - 1, 1.0, 0.0)]
    masks = [column_mask(level) for level in levels]
    for level in levels:
        zero = jnp.zeros((level.cols, LANES), F32)
        level.WZ[0] = zero
        level.U[0] = zero
        level.U[level.rows + 1] = zero
    for ref in (fz0, fz1, fz2):
        ref[0] = jnp.zeros(ref.shape[1:], F32)
        ref[ref.shape[0] - 1] = jnp.zeros(ref.shape[1:], F32)
    guess[0] = jnp.zeros(guess.shape[1:], F32)
    guess[25] = jnp.zeros(guess.shape[1:], F32)
    solved[0] = jnp.zeros(solved.shape[1:], F32)
    solved[n_depth + 1] = jnp.zeros(solved.shape[1:], F32)

    wall.collect()

    for block in (1, 0, 2):
        for (dz, _), copy in ring_inputs:
            if dz == 1 - block:
                copy.wait_recv()
        code = packed[block]
        rows = pl.ds(8 * block, 8)
        temp[rows] = 0.5 + lax.shift_right_logical(code, 16).astype(F32) * (1.5 / 65535.0)
        virgin[rows] = 0.2 + (code & 0xFFFF).astype(F32) * (0.8 / 65535.0)
        if block == 1:
            temp[rows, 8:24] = own_t
            virgin[rows, 8:24] = own_v
        zone = jnp.concatenate([jnp.broadcast_to(zones[block, part], (8, LANES)) for part in range(4)], axis=0)
        inside = masks[0] * row_mask[block]
        props = [jnp.zeros((top.cols, LANES), F32) for _ in range(4)]
        for number in range(n_zones):
            hit = zone == number
            props = [jnp.where(hit, props_ref[kind, number], props[kind]) for kind in range(4)]
        props = [value * inside for value in props]
        for row in range(8 * block, 8 * block + 8, 2):
            rows = pl.ds(row, 2)
            t, v = temp[rows], virgin[rows]
            squared = t * t
            blend = (0.5 + squared) * (0.4 + 0.6 * v)
            rate = 8.0 * v * jnp.exp(-3.0 / t)
            fz0[pl.ds(row + 1, 2)] = props[0] * blend
            fx0[rows] = props[1] * blend
            fy0[rows] = props[2] * blend
            fd0[rows] = (props[3] * (0.5 + v) + 6.0 * rate / squared) * inside
            top.B[rows] = -2.0 * rate * inside

    fields = [(fd0, fx0, fy0, fz0), (fd1, fx1, fy1, fz1), (fd2, fx2, fy2, fz2), (fd3, fx3, fy3, fz3)]
    scratches = (t0, t1, t2)

    for index, level in enumerate(levels):
        fd, fx, fy, fz = fields[index]
        half = 0.5 * 0.25**index
        step = min(4, level.halo_z)
        lane = lax.broadcasted_iota(jnp.int32, (step, level.cols, LANES), 2)
        for row in range(0, level.rows, step):
            rows = pl.ds(row, step)
            inside = masks[index] * row_mask[row // level.halo_z]
            here = fz[pl.ds(row + 1, step)]
            lower = half * (here + fz[rows])
            upper = half * (here + fz[pl.ds(row + 2, step)])
            level.WZ[pl.ds(row + 1, step)] = upper
            across = fx[rows]
            east = half * (across + roll(across, -1, 1))
            west = roll(east, 1, 1)
            level.WX[rows] = east
            along = fy[rows]
            north = 0.5 * (along + jnp.where(lane == LANES - 1, 0.0, roll(along, -1, 2)))
            south = 0.5 * (along + jnp.where(lane == 0, 0.0, roll(along, 1, 2)))
            level.WY[rows] = jnp.where(lane == LANES - 1, 0.0, north)
            centre = fd[rows] + lower + upper + west + east + south + north
            level.C[rows] = centre
            level.WI[rows] = jnp.where((inside > 0.0)[None], OMEGA / centre, 0.0)
        for kind in range(4):
            skip = 1 if kind == 3 else 0
            target_skip = 1 if kind == 3 and index < 2 else 0
            restrict_into(fields[index][kind], skip, scratches[index], fields[index + 1][kind], target_skip)

    half = 0.5 * 0.25**3
    centre_z, centre_x, centre_y = fz3[1, 1:3], fx3[1, 1:3], fy3[1, 1:3]
    lane = lax.broadcasted_iota(jnp.int32, (2, LANES), 1)
    lower = half * (centre_z + fz3[0, 1:3])
    upper = half * (centre_z + fz3[2, 1:3])
    west = half * (centre_x + fx3[1, 0:2])
    east = half * (centre_x + fx3[1, 2:4])
    north = 0.5 * (centre_y + jnp.where(lane == LANES - 1, 0.0, roll(centre_y, -1, 1)))
    south = 0.5 * (centre_y + jnp.where(lane == 0, 0.0, roll(centre_y, 1, 1)))
    centre = fd3[1, 1:3] + lower + upper + west + east + south + north
    for column in range(2):
        coef_own[0, column] = centre[column : column + 1]
        coef_own[1, column] = upper[column : column + 1]

    source_column = {-1: (0, 1), 0: (0, 2), 1: (1, 1)}
    landing_column = {-1: 3, 0: 1, 1: 0}

    def column_copy(phase, dz, dx):
        first, count = source_column[dx]
        if phase == 0:
            src, dst = coef_own.at[:, pl.ds(first, count)], coef_all.at[depth, :, pl.ds(landing_column[dx], count)]
        else:
            src = rhs_own.at[phase - 1, pl.ds(first, count)]
            dst = rhs_all.at[phase - 1, depth, pl.ds(landing_column[dx], count)]
        return pltpu.make_async_remote_copy(
            src_ref=src, dst_ref=dst, send_sem=g_send.at[phase, dz, dx + 1],
            recv_sem=g_recv.at[phase, dz, dx + 1], device_id=at(dz, dx), device_id_type=MESH)

    def each_column(phase, act):
        for dx in (-1, 1):
            act(column_copy(phase, 0, dx))

        def body(dz, carry):
            for dx in (-1, 0, 1):
                act(column_copy(phase, dz, dx))
            return carry

        lax.fori_loop(1, n_depth, body, 0)

    each_column(0, lambda copy: copy.start())
    coef_all[depth, :, 1:3] = coef_own[...]

    wall.add_to(top.B, 8)

    def down(level, scratch, coarse_rhs, chunk):
        for row in range(0, level.rows, chunk):
            res[pl.ds(row, chunk), 0 : level.cols] = residual(level, level.U, row, chunk)
        restrict_into(res.at[:, pl.ds(0, level.cols)], 0, scratch, coarse_rhs, 0)

    def near_copies(cycle):
        pairs = []
        for index, (dz, dx) in enumerate(((-1, 0), (1, 0), (0, -1), (0, 1))):
            side = index % 2
            out, into = (z_out, z_in) if dz else (x_out, x_in)
            pairs.append(pltpu.make_async_remote_copy(
                src_ref=out.at[cycle, side], dst_ref=into.at[cycle, 1 - side],
                send_sem=h_send.at[cycle, index], recv_sem=h_recv.at[cycle, index],
                device_id=at(dz, dx), device_id_type=MESH))
        return pairs

    def run_cycle(cycle, last):
        down(top, t0, mid.B, 4)
        mid.U[1:13] = mid.WI[...] * mid.B[...]
        down(mid, t1, low.B, 4)
        low.U[1:7] = low.WI[...] * low.B[...]
        down(low, t2, b3, 6)
        for column in range(2):
            rhs_own[cycle, column] = b3[1, 1 + column : 2 + column]
        each_column(1 + cycle, lambda copy: copy.start())
        z_out[cycle, 0, 0] = low.B[2]
        z_out[cycle, 0, 1] = low.U[4]
        z_out[cycle, 1, 0] = low.B[3]
        z_out[cycle, 1, 1] = low.U[3]
        for row in range(4):
            x_out[cycle, 0, row] = low.U[2 + row, 3:4]
            x_out[cycle, 1, row] = low.U[2 + row, 4:5]
        near = near_copies(cycle)
        for copy in near:
            copy.start()
        rhs_all[cycle, depth, 1:3] = rhs_own[cycle]

        if cycle == 0:
            for _, copy in ring_inputs:
                copy.wait_send()
            each_column(0, lambda copy: copy.wait_send())
            wall.finish()
        else:
            for copy in ring_guess:
                copy.wait_send()
            each_column(1, lambda copy: copy.wait_send())
            for copy in near_copies(0):
                copy.wait_send()

        if cycle == 0:
            each_column(0, lambda copy: copy.wait_recv())
            inv = 1.0 / coef_all[0, 0]
            inverse[0] = inv
            ratio[0] = coef_all[0, 1] * inv
            for row in range(1, n_depth):
                inv = 1.0 / (coef_all[row, 0] - coef_all[row - 1, 1] * ratio[row - 1])
                inverse[row] = inv
                ratio[row] = coef_all[row, 1] * inv

        for copy in near:
            copy.wait_recv()
        low.B[1] = z_in[cycle, 0, 0]
        low.B[4] = z_in[cycle, 1, 0]
        low.U[2] = low.WI[1] * low.B[1]
        low.U[5] = low.WI[4] * low.B[4]
        low.U[1] = z_in[cycle, 0, 1] * (masks[2] * row_mask[0])
        low.U[6] = z_in[cycle, 1, 1] * (masks[2] * row_mask[2])
        for row in range(4):
            block = (0, 1, 1, 2)[row]
            first = jnp.where(surf > 0, 1.0, 0.0) * row_mask[block]
            final = jnp.where(surf < n_surf - 1, 1.0, 0.0) * row_mask[block]
            low.U[2 + row, 0:1] = x_in[cycle, 0, row] * first
            low.U[2 + row, 7:8] = x_in[cycle, 1, row] * final

        each_column(1 + cycle, lambda copy: copy.wait_recv())
        value = rhs_all[cycle, 0] * inverse[0]
        values = [value]
        for row in range(1, n_depth):
            value = (rhs_all[cycle, row] + coef_all[row - 1, 1] * value) * inverse[row]
            values.append(value)
        later = values[-1]
        solved[n_depth] = later
        for row in range(n_depth - 2, -1, -1):
            later = values[row] + ratio[row] * later
            solved[row + 1] = later
        for row in range(3):
            for column in range(4):
                value = solved[depth + row, column]
                if column == 0:
                    value = value * jnp.where(surf > 0, 1.0, 0.0)
                if column == 3:
                    value = value * jnp.where(surf < n_surf - 1, 1.0, 0.0)
                e2[row, 2 * column : 2 * column + 2] = jnp.broadcast_to(value, (2, LANES))
        for row in range(3):
            wide = e2[row]
            low.U[1 + 2 * row] = low.U[1 + 2 * row] + wide
            low.U[2 + 2 * row] = low.U[2 + 2 * row] + wide
        v2[...] = low.U[1:7] + low.WI[...] * residual(low, low.U, 0, 6)
        prolong_onto(mid, v2, t1, 2, 8)
        v1[2:10] = mid.U[3:11] + mid.WI[2:10] * residual(mid, mid.U, 2, 8)
        prolong_onto(top, v1, t0, 6, 12)
        for row in range(8, 16, 4):
            rows = pl.ds(row, 4)
            new = top.U[pl.ds(row + 1, 4)] + top.WI[rows] * residual(top, top.U, row, 4)
            if last:
                out_ref[pl.ds(row - 8, 4)] = new[:, 8:24]
            else:
                guess[pl.ds(row + 1, 4), 8:24] = new[:, 8:24]

    top.U[1:25] = top.WI[...] * top.B[...]
    run_cycle(0, False)
    for copy in ring_guess:
        copy.start()
    for copy in ring_guess:
        copy.wait_recv()
    for block in range(3):
        rows = pl.ds(1 + 8 * block, 8)
        if block == 1:
            for columns, inside in ((slice(0, 8), surf > 0), (slice(24, 32), surf < n_surf - 1)):
                guess[rows, columns] = guess[rows, columns] * jnp.where(inside, 1.0, 0.0)
        else:
            guess[rows] = guess[rows] * (masks[0] * row_mask[block])
    for row in range(0, 24, 4):
        rows, padded = pl.ds(row, 4), pl.ds(row + 1, 4)
        top.U[padded] = guess[padded] + top.WI[rows] * residual(top, guess, row, 4)
    run_cycle(1, True)

    each_column(2, lambda copy: copy.wait_send())
    for copy in near_copies(1):
        copy.wait_send()


def per_device(n_surf, n_depth, temp_old, virgin, zone, zone_props, gas_flux, gas_owner, gas_cell):
    width = temp_old.shape[1]
    span = min(GROUP, n_surf // 2)
    groups = n_surf // span
    rows = gas_flux.shape[0]
    dma = pltpu.SemaphoreType.DMA

    def box(*shape):
        return pltpu.VMEM((*shape, LANES), F32)

    def fields(index):
        r, c = 24 >> index, 32 >> index
        return [box(r, c), box(r, c), box(r, c), box(r if index == 3 else r + 2, c)]

    def level(index):
        r, c = 24 >> index, 32 >> index
        return [box(r, c)] * 5 + [box(r + 2, c)] * 2

    def ints(*shape):
        return pltpu.VMEM((*shape, LANES), jnp.int32)

    wall = [
        pltpu.VMEM((rows, LANES), jnp.bfloat16), ints(1),
        pltpu.VMEM((groups, rows, LANES), jnp.bfloat16), ints(groups, 1),
        box(span * width + width), box(span, 2 * width),
        dma((2, groups)), dma((2, groups)), dma((span,)), dma((span,)),
    ]
    scratch = [
        box(*temp_old.shape[:2]), box(*temp_old.shape[:2]), ints(width), pltpu.SMEM(zone_props.shape, F32),
        ints(1), ints(1), dma((7,)), wall,
        pltpu.VMEM((3, 8, 32, LANES), jnp.int32), ints(3, 4, 1), box(26, 32), box(24, 32), box(24, 32),
        *fields(0), *fields(1), *fields(2), *fields(3),
        level(0), level(1), level(2),
        box(24, 32), box(12, 32), box(6, 16), box(3, 8), box(12, 16), box(6, 8), box(3, 4),
        box(2, 2, 1), box(n_depth, 2, 4, 1), box(2, 2, 1), box(2, n_depth, 4, 1),
        box(n_depth, 4, 1), box(n_depth, 4, 1), box(n_depth + 2, 4, 1), box(3, 8),
        box(2, 2, 2, 8), box(2, 2, 2, 8), box(2, 2, 4, 1), box(2, 2, 4, 1),
        dma((20,)), dma((20,)), dma((16,)), dma((16,)),
        dma((3, n_depth, 3)), dma((3, n_depth, 3)), dma((2, 4)), dma((2, 4)),
    ]
    return pl.pallas_call(
        functools.partial(cycles_kernel, n_surf, n_depth, zone_props.shape[1], groups, span),
        out_shape=jax.ShapeDtypeStruct(temp_old.shape, F32),
        in_specs=[pl.BlockSpec(memory_space=pltpu.HBM)] * 7,
        out_specs=pl.BlockSpec(memory_space=pltpu.VMEM),
        scratch_shapes=scratch,
        compiler_params=pltpu.CompilerParams(
            collective_id=0, has_side_effects=True, vmem_limit_bytes=48 * 1024 * 1024),
        name="cycles",
    )(*[pltpu.with_memory_space_constraint(a, pltpu.HBM) for a in (temp_old, virgin, zone, zone_props, gas_flux, gas_owner.reshape(1, rows), gas_cell.reshape(1, rows))])


def solution(mesh):
    return jax.shard_map(
        functools.partial(per_device, mesh.shape["surf"], mesh.shape["depth"]),
        mesh=mesh,
        in_specs=(
            P("depth", "surf", None),
            P("depth", "surf", None),
            P("depth", "surf", None),
            P(),
            P("surf", None),
            P("surf", None),
            P("surf"),
        ),
        out_specs=P("depth", "surf", None),
        check_vma=False,
    )
```

```python
import functools

import jax
import jax.numpy as jnp
from jax import lax
from jax.experimental import pallas as pl
from jax.experimental.pallas import tpu as pltpu
from jax.sharding import PartitionSpec as P

MESH = pl.DeviceIdType.MESH
F32 = jnp.float32
OMEGA = 0.8
LANES = 128
GROUP = 16


def roll(value, shift, axis):
    return pltpu.roll(value, shift % value.shape[axis], axis)


class Wall:
    def __init__(self, groups, span, width, refs):
        (self.flux, self.target, self.flux_all, self.target_all, self.partial, self.parts,
         self.send1, self.recv1, self.send2, self.recv2) = refs
        self.groups, self.span, self.width = groups, span, width
        surf, self.depth = lax.axis_index("surf"), lax.axis_index("depth")
        self.group, self.member = surf // span, lax.rem(surf, span)
        self.collects = (self.depth < 2) & (lax.rem(self.group, 2) == self.depth)
        self.owner = self.depth == 0

    def is_self(self, other):
        return self.owner & (lax.rem(self.group, 2) == 0) & (other == self.member)

    def copies1(self, to_group, slot):
        where = (to_group * self.span + self.member, self.depth)
        return [
            pltpu.make_async_remote_copy(
                src_ref=src, dst_ref=dst.at[slot], send_sem=self.send1.at[kind, to_group],
                recv_sem=self.recv1.at[kind, slot], device_id=where, device_id_type=MESH)
            for kind, (src, dst) in enumerate(((self.flux, self.flux_all), (self.target, self.target_all)))
        ]

    def rows_for(self, member):
        return self.partial.at[pl.ds(pl.multiple_of(member * self.width, 8), 2 * self.width)]

    def copy2(self, to_member, slot):
        return pltpu.make_async_remote_copy(
            src_ref=self.rows_for(to_member), dst_ref=self.parts.at[slot],
            send_sem=self.send2.at[to_member], recv_sem=self.recv2.at[slot],
            device_id=(self.group * self.span + to_member, 0), device_id_type=MESH)

    def greet(self, barrier):
        @pl.when(self.collects)
        def _():
            def body(other, carry):
                @pl.when(other != self.group)
                def _():
                    pl.semaphore_signal(
                        barrier, inc=1, device_id=(other * self.span + self.member, self.depth), device_id_type=MESH)
                return carry
            lax.fori_loop(0, self.groups, body, 0)

        @pl.when(self.owner)
        def _():
            def body(other, carry):
                @pl.when(jnp.logical_not(self.is_self(other)))
                def _():
                    pl.semaphore_signal(
                        barrier, inc=1, device_id=(self.group * self.span + other, lax.rem(self.group, 2)),
                        device_id_type=MESH)
                return carry
            lax.fori_loop(0, self.span, body, 0)

    def greetings(self):
        collecting = jnp.where(self.collects, 1, 0)
        from_owners = collecting * (self.span - jnp.where(self.owner, 1, 0))
        return jnp.where(self.depth < 2, self.groups // 2 - collecting, 0) + from_owners

    def each_group(self, act):
        @pl.when(self.depth < 2)
        def _():
            def body(half, carry):
                to_group = 2 * half + self.depth
                @pl.when(to_group != self.group)
                def _():
                    for copy in self.copies1(to_group, self.group):
                        act(copy)
                return carry
            lax.fori_loop(0, self.groups // 2, body, 0)

    def each_member(self, act):
        def body(member, carry):
            @pl.when(jnp.logical_not(self.is_self(member)))
            def _():
                act(self.copy2(member, self.member))
            return carry
        lax.fori_loop(0, self.span, body, 0)

    def collect(self):
        @pl.when(self.collects)
        def _():
            self.flux_all[self.group] = self.flux[...]
            self.target_all[self.group] = self.target[...]
            self.partial[...] = jnp.zeros_like(self.partial)
            rows = self.partial.shape[0]
            first = self.group * (self.span * self.width) - self.width // 2
            ids = first + lax.broadcasted_iota(jnp.int32, (rows, LANES), 0)

            def add(other, carry):
                @pl.when(other != self.group)
                def _():
                    for copy in self.copies1(other, other):
                        copy.wait_recv()
                placing = jnp.where(ids == self.target_all[other], 1.0, 0.0).astype(jnp.bfloat16)
                self.partial[...] += jnp.dot(placing, self.flux_all[other], preferred_element_type=F32)
                return carry
            lax.fori_loop(0, self.groups, add, 0)

            @pl.when(self.is_self(self.member))
            def _():
                self.parts[self.member] = self.rows_for(self.member)[...]
            self.each_member(lambda copy: copy.start())

    def add_to(self, source, row):
        @pl.when(self.owner)
        def _():
            def body(other, carry):
                @pl.when(jnp.logical_not(self.is_self(other)))
                def _():
                    self.copy2(other, other).wait_recv()
                source[row] = source[row] + self.parts[other]
                return carry
            lax.fori_loop(0, self.span, body, 0)

    def finish(self):
        self.each_group(lambda copy: copy.wait_send())

        @pl.when(self.collects)
        def _():
            self.each_member(lambda copy: copy.wait_send())


SIDES = [(-1, 0), (1, 0), (-1, -1), (-1, 1), (1, -1), (1, 1), (0, -1), (0, 1)]


class Level:
    def __init__(self, refs, halo_z, halo_x):
        self.C, self.WX, self.WY, self.WI, self.B, self.WZ, self.U = refs
        self.rows, self.cols = self.C.shape[0], self.C.shape[1]
        self.halo_z, self.halo_x = halo_z, halo_x


def residual(level, field, first, count):
    here, up, down = (pl.ds(first + shift, count) for shift in (1, 2, 0))
    own = pl.ds(first, count)
    mid = field[here]
    wx, wy = level.WX[own], level.WY[own]
    total = level.B[own] - level.C[own] * mid
    total = total + level.WZ[here] * field[up] + level.WZ[down] * field[down]
    total = total + wx * roll(mid, -1, 1) + roll(wx * mid, 1, 1)
    return total + wy * roll(mid, -1, 2) + roll(wy * mid, 1, 2)


def restrict_into(source, skip, scratch, target, target_skip):
    rows, cols = scratch.shape[0], scratch.shape[1]
    for row in range(rows):
        scratch[row] = source[skip + 2 * row] + source[skip + 2 * row + 1]
    even = scratch[:, pl.ds(0, cols // 2, stride=2), :]
    odd = scratch[:, pl.ds(1, cols // 2, stride=2), :]
    target[pl.ds(target_skip, rows)] = 0.25 * (even + odd)


def prolong_onto(level, coarse, scratch, first, count):
    cols = scratch.shape[1]
    low, number = first // 2, count // 2
    part = coarse[pl.ds(low, number)]
    scratch[pl.ds(low, number), pl.ds(0, cols // 2, stride=2), :] = part
    scratch[pl.ds(low, number), pl.ds(1, cols // 2, stride=2), :] = part
    for row in range(low, low + number):
        wide = scratch[row]
        level.U[1 + 2 * row] = level.U[1 + 2 * row] + wide
        level.U[2 + 2 * row] = level.U[2 + 2 * row] + wide


def cycles_kernel(n_surf, n_depth, n_zones, groups, span,
                  temp_hbm, virgin_hbm, zone_hbm, props_hbm, flux_hbm, owner_hbm, cell_hbm, out_ref,
                  temp_ref, virgin_ref, zone_ref, props_ref, owner_ref, cell_ref, in_sem, wall_refs,
                  packed, zones, guess, temp, virgin,
                  fd0, fx0, fy0, fz0, fd1, fx1, fy1, fz1, fd2, fx2, fy2, fz2, fd3, fx3, fy3, fz3,
                  l0, l1, l2, res, t0, t1, t2, v1, v2, b3,
                  coef_own, coef_all, rhs_own, rhs_all, ratio, inverse, solved, e2,
                  z_out, z_in, x_out, x_in,
                  s_send, s_recv, e_send, e_recv, g_send, g_recv, h_send, h_recv):
    surf, depth = lax.axis_index("surf"), lax.axis_index("depth")

    def at(dz, dx):
        return (lax.rem(surf + dx + n_surf, n_surf), lax.rem(depth + dz + n_depth, n_depth))

    levels = [Level(refs, 8 >> index, 8 >> index) for index, refs in enumerate((l0, l1, l2))]
    top, mid, low = levels

    width = out_ref.shape[1]
    wall = Wall(groups, span, width, wall_refs)
    inputs = [
        pltpu.make_async_copy(src, dst, in_sem.at[index])
        for index, (src, dst) in enumerate((
            (temp_hbm, temp_ref), (virgin_hbm, virgin_ref), (zone_hbm.at[0], zone_ref), (flux_hbm, wall.flux),
            (owner_hbm, owner_ref), (cell_hbm, cell_ref), (props_hbm, props_ref)))
    ]
    for copy in inputs:
        copy.start()
    for columns in (pl.ds(0, 8), pl.ds(24, 8)):
        for block in (0, 2):
            packed[block, :, columns] = jnp.zeros((8, 8, LANES), jnp.int32)
            guess[pl.ds(1 + 8 * block, 8), columns] = jnp.zeros((8, 8, LANES), F32)

    barrier = pltpu.get_barrier_semaphore()

    def greet(step, carry):
        dz = n_depth // 2 + jnp.where(lax.rem(step, 2) == 1, (step + 1) // 2, -(step // 2))
        for dx in (-1, 0, 1):
            pl.semaphore_signal(barrier, inc=1, device_id=at(dz, dx), device_id_type=MESH)
        return carry

    lax.fori_loop(0, n_depth - 1, greet, 0)
    for dx in (-1, 1):
        pl.semaphore_signal(barrier, inc=1, device_id=at(0, dx), device_id_type=MESH)
    wall.greet(barrier)
    for copy in inputs:
        copy.wait()
    wall.target[...] = owner_ref[...] * width + cell_ref[...]

    own_t = temp_ref[...]
    own_v = virgin_ref[...]
    code_t = ((own_t - 0.5) * (65535.0 / 1.5) + 0.5).astype(jnp.int32)
    code_v = ((own_v - 0.2) * (65535.0 / 0.8) + 0.5).astype(jnp.int32)
    packed[1, :, 8:24] = jnp.left_shift(code_t, 16) | code_v
    for half in range(2):
        zones[1, 1 + half] = zone_ref[8 * half : 8 * half + 1]
    pl.semaphore_wait(barrier, 3 * n_depth - 1 + wall.greetings())

    src_x = {-1: (8, 8), 0: (8, 16), 1: (16, 8)}
    dst_x = {-1: 24, 0: 8, 1: 0}

    def ring_copy(index, ref_src, ref_dst, send, recv, dz, dx):
        return pltpu.make_async_remote_copy(
            src_ref=ref_src, dst_ref=ref_dst, send_sem=send.at[index], recv_sem=recv.at[index],
            device_id=at(dz, dx), device_id_type=MESH)

    def pieces(sizes, dz, dx):
        found = []
        for first_row, last_row, columns in sizes:
            first = first_row if dz < 0 else 9 - last_row
            count = last_row - first_row + 1
            low, _ = src_x[dx]
            skip = 0 if dx < 0 else 8 - columns
            found.append((first, count, low + skip, dst_x[dx] + skip, columns))
        return found

    def setup_copies():
        copies = []
        for dz, dx in SIDES:
            if dz and dx:
                parts = pieces(((1, 4, 8), (5, 8, 4)), dz, dx)
            else:
                parts = [(1, 8, src_x[dx][0], dst_x[dx], src_x[dx][1])]
            for row, rows, src, dst, columns in parts:
                copies.append(((dz, dx), ring_copy(
                    len(copies), packed.at[1, pl.ds(row - 1, rows), pl.ds(src, columns)],
                    packed.at[1 - dz, pl.ds(row - 1, rows), pl.ds(dst, columns)], s_send, s_recv, dz, dx)))
            src, count, dst = {-1: (1, 1, 3), 0: (1, 2, 1), 1: (2, 1, 0)}[dx]
            copies.append(((dz, dx), ring_copy(
                len(copies), zones.at[1, pl.ds(src, count)], zones.at[1 - dz, pl.ds(dst, count)],
                s_send, s_recv, dz, dx)))
        return copies

    def guess_copies():
        copies = []
        for dz, dx in SIDES:
            if dz and dx:
                parts = pieces(((1, 2, 7), (3, 4, 5), (5, 7, 3)), dz, dx)
            else:
                parts = [(1, 8, src_x[dx][0], dst_x[dx], src_x[dx][1])]
            for row, rows, src, dst, columns in parts:
                copies.append(ring_copy(
                    len(copies), guess.at[pl.ds(8 + row, rows), pl.ds(src, columns)],
                    guess.at[pl.ds(8 * (1 - dz) + row, rows), pl.ds(dst, columns)], e_send, e_recv, dz, dx))
        return copies

    ring_inputs, ring_guess = setup_copies(), guess_copies()
    wall.each_group(lambda copy: copy.start())
    for _, copy in ring_inputs:
        copy.start()

    def column_mask(level):
        column = lax.broadcasted_iota(jnp.int32, (level.cols, LANES), 0)
        first, last = level.halo_x, level.cols - level.halo_x
        inside = ((column >= first) | (surf > 0)) & ((column < last) | (surf < n_surf - 1))
        return jnp.where(inside, 1.0, 0.0)

    row_mask = [jnp.where(depth > 0, 1.0, 0.0), jnp.float32(1.0), jnp.where(depth < n_depth - 1, 1.0, 0.0)]
    masks = [column_mask(level) for level in levels]
    for level in levels:
        zero = jnp.zeros((level.cols, LANES), F32)
        level.WZ[0] = zero
        level.U[0] = zero
        level.U[level.rows + 1] = zero
    for ref in (fz0, fz1, fz2):
        ref[0] = jnp.zeros(ref.shape[1:], F32)
        ref[ref.shape[0] - 1] = jnp.zeros(ref.shape[1:], F32)
    guess[0] = jnp.zeros(guess.shape[1:], F32)
    guess[25] = jnp.zeros(guess.shape[1:], F32)
    for row in (0, 1, 22, 23):
        res[row] = jnp.zeros(res.shape[1:], F32)
    solved[0] = jnp.zeros(solved.shape[1:], F32)
    solved[n_depth + 1] = jnp.zeros(solved.shape[1:], F32)

    wall.collect()

    for block in (1, 0, 2):
        for (dz, _), copy in ring_inputs:
            if dz == 1 - block:
                copy.wait_recv()
        code = packed[block]
        rows = pl.ds(8 * block, 8)
        temp[rows] = 0.5 + lax.shift_right_logical(code, 16).astype(F32) * (1.5 / 65535.0)
        virgin[rows] = 0.2 + (code & 0xFFFF).astype(F32) * (0.8 / 65535.0)
        if block == 1:
            temp[rows, 8:24] = own_t
            virgin[rows, 8:24] = own_v
        zone = jnp.concatenate([jnp.broadcast_to(zones[block, part], (8, LANES)) for part in range(4)], axis=0)
        inside = masks[0] * row_mask[block]
        props = [jnp.zeros((top.cols, LANES), F32) for _ in range(4)]
        for number in range(n_zones):
            hit = zone == number
            props = [jnp.where(hit, props_ref[kind, number], props[kind]) for kind in range(4)]
        props = [value * inside for value in props]
        for row in range(8 * block, 8 * block + 8, 2):
            rows = pl.ds(row, 2)
            t, v = temp[rows], virgin[rows]
            squared = t * t
            blend = (0.5 + squared) * (0.4 + 0.6 * v)
            rate = 8.0 * v * jnp.exp(-3.0 / t)
            fz0[pl.ds(row + 1, 2)] = props[0] * blend
            fx0[rows] = props[1] * blend
            fy0[rows] = props[2] * blend
            fd0[rows] = (props[3] * (0.5 + v) + 6.0 * rate / squared) * inside
            top.B[rows] = -2.0 * rate * inside

    fields = [(fd0, fx0, fy0, fz0), (fd1, fx1, fy1, fz1), (fd2, fx2, fy2, fz2), (fd3, fx3, fy3, fz3)]
    scratches = (t0, t1, t2)

    for index, level in enumerate(levels):
        fd, fx, fy, fz = fields[index]
        half = 0.5 * 0.25**index
        step = min(4, level.halo_z)
        lane = lax.broadcasted_iota(jnp.int32, (step, level.cols, LANES), 2)
        for row in range(0, level.rows, step):
            rows = pl.ds(row, step)
            inside = masks[index] * row_mask[row // level.halo_z]
            here = fz[pl.ds(row + 1, step)]
            lower = half * (here + fz[rows])
            upper = half * (here + fz[pl.ds(row + 2, step)])
            level.WZ[pl.ds(row + 1, step)] = upper
            across = fx[rows]
            east = half * (across + roll(across, -1, 1))
            west = roll(east, 1, 1)
            level.WX[rows] = east
            along = fy[rows]
            north = 0.5 * (along + jnp.where(lane == LANES - 1, 0.0, roll(along, -1, 2)))
            south = 0.5 * (along + jnp.where(lane == 0, 0.0, roll(along, 1, 2)))
            level.WY[rows] = jnp.where(lane == LANES - 1, 0.0, north)
            centre = fd[rows] + lower + upper + west + east + south + north
            level.C[rows] = centre
            level.WI[rows] = jnp.where((inside > 0.0)[None], OMEGA / centre, 0.0)
        for kind in range(4):
            skip = 1 if kind == 3 else 0
            target_skip = 1 if kind == 3 and index < 2 else 0
            restrict_into(fields[index][kind], skip, scratches[index], fields[index + 1][kind], target_skip)

    half = 0.5 * 0.25**3
    centre_z, centre_x, centre_y = fz3[1, 1:3], fx3[1, 1:3], fy3[1, 1:3]
    lane = lax.broadcasted_iota(jnp.int32, (2, LANES), 1)
    lower = half * (centre_z + fz3[0, 1:3])
    upper = half * (centre_z + fz3[2, 1:3])
    west = half * (centre_x + fx3[1, 0:2])
    east = half * (centre_x + fx3[1, 2:4])
    north = 0.5 * (centre_y + jnp.where(lane == LANES - 1, 0.0, roll(centre_y, -1, 1)))
    south = 0.5 * (centre_y + jnp.where(lane == 0, 0.0, roll(centre_y, 1, 1)))
    centre = fd3[1, 1:3] + lower + upper + west + east + south + north
    for column in range(2):
        coef_own[0, column] = centre[column : column + 1]
        coef_own[1, column] = upper[column : column + 1]

    source_column = {-1: (0, 1), 0: (0, 2), 1: (1, 1)}
    landing_column = {-1: 3, 0: 1, 1: 0}

    def column_copy(phase, dz, dx):
        first, count = source_column[dx]
        if phase == 0:
            src, dst = coef_own.at[:, pl.ds(first, count)], coef_all.at[depth, :, pl.ds(landing_column[dx], count)]
        else:
            src = rhs_own.at[phase - 1, pl.ds(first, count)]
            dst = rhs_all.at[phase - 1, depth, pl.ds(landing_column[dx], count)]
        return pltpu.make_async_remote_copy(
            src_ref=src, dst_ref=dst, send_sem=g_send.at[phase, dz, dx + 1],
            recv_sem=g_recv.at[phase, dz, dx + 1], device_id=at(dz, dx), device_id_type=MESH)

    def each_column(phase, act):
        for dx in (-1, 1):
            act(column_copy(phase, 0, dx))

        def body(dz, carry):
            for dx in (-1, 0, 1):
                act(column_copy(phase, dz, dx))
            return carry

        lax.fori_loop(1, n_depth, body, 0)

    each_column(0, lambda copy: copy.start())
    coef_all[depth, :, 1:3] = coef_own[...]

    wall.add_to(top.B, 8)

    def down(level, scratch, coarse_rhs, chunk):
        edge = 2 if level is top else 0
        for row in range(edge, level.rows - edge, chunk):
            res[pl.ds(row, chunk), 0 : level.cols] = residual(level, level.U, row, chunk)
        restrict_into(res.at[:, pl.ds(0, level.cols)], 0, scratch, coarse_rhs, 0)

    def near_copies(cycle):
        pairs = []
        for index, (dz, dx) in enumerate(((-1, 0), (1, 0), (0, -1), (0, 1))):
            side = index % 2
            out, into = (z_out, z_in) if dz else (x_out, x_in)
            pairs.append(pltpu.make_async_remote_copy(
                src_ref=out.at[cycle, side], dst_ref=into.at[cycle, 1 - side],
                send_sem=h_send.at[cycle, index], recv_sem=h_recv.at[cycle, index],
                device_id=at(dz, dx), device_id_type=MESH))
        return pairs

    def run_cycle(cycle, last):
        down(top, t0, mid.B, 4)
        mid.U[1:13] = mid.WI[...] * mid.B[...]
        down(mid, t1, low.B, 4)
        low.U[1:7] = low.WI[...] * low.B[...]
        down(low, t2, b3, 6)
        for column in range(2):
            rhs_own[cycle, column] = b3[1, 1 + column : 2 + column]
        each_column(1 + cycle, lambda copy: copy.start())
        z_out[cycle, 0, 0] = low.B[2]
        z_out[cycle, 0, 1] = low.U[4]
        z_out[cycle, 1, 0] = low.B[3]
        z_out[cycle, 1, 1] = low.U[3]
        for row in range(4):
            x_out[cycle, 0, row] = low.U[2 + row, 3:4]
            x_out[cycle, 1, row] = low.U[2 + row, 4:5]
        near = near_copies(cycle)
        for copy in near:
            copy.start()
        rhs_all[cycle, depth, 1:3] = rhs_own[cycle]

        if cycle == 0:
            for _, copy in ring_inputs:
                copy.wait_send()
            each_column(0, lambda copy: copy.wait_send())
            wall.finish()
        else:
            for copy in ring_guess:
                copy.wait_send()
            each_column(1, lambda copy: copy.wait_send())
            for copy in near_copies(0):
                copy.wait_send()

        if cycle == 0:
            each_column(0, lambda copy: copy.wait_recv())
            inv = 1.0 / coef_all[0, 0]
            inverse[0] = inv
            ratio[0] = coef_all[0, 1] * inv
            for row in range(1, n_depth):
                inv = 1.0 / (coef_all[row, 0] - coef_all[row - 1, 1] * ratio[row - 1])
                inverse[row] = inv
                ratio[row] = coef_all[row, 1] * inv

        for copy in near:
            copy.wait_recv()
        low.B[1] = z_in[cycle, 0, 0]
        low.B[4] = z_in[cycle, 1, 0]
        low.U[2] = low.WI[1] * low.B[1]
        low.U[5] = low.WI[4] * low.B[4]
        low.U[1] = z_in[cycle, 0, 1] * (masks[2] * row_mask[0])
        low.U[6] = z_in[cycle, 1, 1] * (masks[2] * row_mask[2])
        for row in range(4):
            block = (0, 1, 1, 2)[row]
            first = jnp.where(surf > 0, 1.0, 0.0) * row_mask[block]
            final = jnp.where(surf < n_surf - 1, 1.0, 0.0) * row_mask[block]
            low.U[2 + row, 0:1] = x_in[cycle, 0, row] * first
            low.U[2 + row, 7:8] = x_in[cycle, 1, row] * final

        each_column(1 + cycle, lambda copy: copy.wait_recv())
        value = rhs_all[cycle, 0] * inverse[0]
        values = [value]
        for row in range(1, n_depth):
            value = (rhs_all[cycle, row] + coef_all[row - 1, 1] * value) * inverse[row]
            values.append(value)
        later = values[-1]
        solved[n_depth] = later
        for row in range(n_depth - 2, -1, -1):
            later = values[row] + ratio[row] * later
            solved[row + 1] = later
        for row in range(3):
            for column in range(4):
                value = solved[depth + row, column]
                if column == 0:
                    value = value * jnp.where(surf > 0, 1.0, 0.0)
                if column == 3:
                    value = value * jnp.where(surf < n_surf - 1, 1.0, 0.0)
                e2[row, 2 * column : 2 * column + 2] = jnp.broadcast_to(value, (2, LANES))
        for row in range(3):
            wide = e2[row]
            low.U[1 + 2 * row] = low.U[1 + 2 * row] + wide
            low.U[2 + 2 * row] = low.U[2 + 2 * row] + wide
        v2[...] = low.U[1:7] + low.WI[...] * residual(low, low.U, 0, 6)
        prolong_onto(mid, v2, t1, 2, 8)
        v1[2:10] = mid.U[3:11] + mid.WI[2:10] * residual(mid, mid.U, 2, 8)
        prolong_onto(top, v1, t0, 6, 12)
        for row in range(8, 16, 4):
            rows = pl.ds(row, 4)
            new = top.U[pl.ds(row + 1, 4)] + top.WI[rows] * residual(top, top.U, row, 4)
            if last:
                out_ref[pl.ds(row - 8, 4)] = new[:, 8:24]
            else:
                guess[pl.ds(row + 1, 4), 8:24] = new[:, 8:24]

    top.U[1:25] = top.WI[...] * top.B[...]
    run_cycle(0, False)
    for copy in ring_guess:
        copy.start()
    for copy in ring_guess:
        copy.wait_recv()
    for block in range(3):
        rows = pl.ds(1 + 8 * block, 8)
        if block == 1:
            for columns, inside in ((slice(0, 8), surf > 0), (slice(24, 32), surf < n_surf - 1)):
                guess[rows, columns] = guess[rows, columns] * jnp.where(inside, 1.0, 0.0)
        else:
            guess[rows] = guess[rows] * (masks[0] * row_mask[block])
    for row in range(0, 24, 4):
        rows, padded = pl.ds(row, 4), pl.ds(row + 1, 4)
        top.U[padded] = guess[padded] + top.WI[rows] * residual(top, guess, row, 4)
    run_cycle(1, True)

    each_column(2, lambda copy: copy.wait_send())
    for copy in near_copies(1):
        copy.wait_send()


def per_device(n_surf, n_depth, temp_old, virgin, zone, zone_props, gas_flux, gas_owner, gas_cell):
    width = temp_old.shape[1]
    span = min(GROUP, n_surf // 2)
    groups = n_surf // span
    rows = gas_flux.shape[0]
    dma = pltpu.SemaphoreType.DMA

    def box(*shape):
        return pltpu.VMEM((*shape, LANES), F32)

    def fields(index):
        r, c = 24 >> index, 32 >> index
        return [box(r, c), box(r, c), box(r, c), box(r if index == 3 else r + 2, c)]

    def level(index):
        r, c = 24 >> index, 32 >> index
        return [box(r, c)] * 5 + [box(r + 2, c)] * 2

    def ints(*shape):
        return pltpu.VMEM((*shape, LANES), jnp.int32)

    wall = [
        pltpu.VMEM((rows, LANES), jnp.bfloat16), ints(1),
        pltpu.VMEM((groups, rows, LANES), jnp.bfloat16), ints(groups, 1),
        box(span * width + width), box(span, 2 * width),
        dma((2, groups)), dma((2, groups)), dma((span,)), dma((span,)),
    ]
    scratch = [
        box(*temp_old.shape[:2]), box(*temp_old.shape[:2]), ints(width), pltpu.SMEM(zone_props.shape, F32),
        ints(1), ints(1), dma((7,)), wall,
        pltpu.VMEM((3, 8, 32, LANES), jnp.int32), ints(3, 4, 1), box(26, 32), box(24, 32), box(24, 32),
        *fields(0), *fields(1), *fields(2), *fields(3),
        level(0), level(1), level(2),
        box(24, 32), box(12, 32), box(6, 16), box(3, 8), box(12, 16), box(6, 8), box(3, 4),
        box(2, 2, 1), box(n_depth, 2, 4, 1), box(2, 2, 1), box(2, n_depth, 4, 1),
        box(n_depth, 4, 1), box(n_depth, 4, 1), box(n_depth + 2, 4, 1), box(3, 8),
        box(2, 2, 2, 8), box(2, 2, 2, 8), box(2, 2, 4, 1), box(2, 2, 4, 1),
        dma((20,)), dma((20,)), dma((16,)), dma((16,)),
        dma((3, n_depth, 3)), dma((3, n_depth, 3)), dma((2, 4)), dma((2, 4)),
    ]
    return pl.pallas_call(
        functools.partial(cycles_kernel, n_surf, n_depth, zone_props.shape[1], groups, span),
        out_shape=jax.ShapeDtypeStruct(temp_old.shape, F32),
        in_specs=[pl.BlockSpec(memory_space=pltpu.HBM)] * 7,
        out_specs=pl.BlockSpec(memory_space=pltpu.VMEM),
        scratch_shapes=scratch,
        compiler_params=pltpu.CompilerParams(
            collective_id=0, has_side_effects=True, vmem_limit_bytes=48 * 1024 * 1024),
        name="cycles",
    )(*[pltpu.with_memory_space_constraint(a, pltpu.HBM) for a in (temp_old, virgin, zone, zone_props, gas_flux, gas_owner.reshape(1, rows), gas_cell.reshape(1, rows))])


def solution(mesh):
    return jax.shard_map(
        functools.partial(per_device, mesh.shape["surf"], mesh.shape["depth"]),
        mesh=mesh,
        in_specs=(
            P("depth", "surf", None),
            P("depth", "surf", None),
            P("depth", "surf", None),
            P(),
            P("surf", None),
            P("surf", None),
            P("surf"),
        ),
        out_specs=P("depth", "surf", None),
        check_vma=False,
    )
```
